32 devices in a mesh: dp: 4 (over y, x), seq: 8 (over z, core).
Axes of the slice: x: 2, y: 2, z: 4, core: 2. Of those that a mesh axis runs over, the one named last changes fastest.
Arguments:
- hidden_in: bfloat16 [8, 4096, 2048], P('dp', 'seq'), may hold values from -6 to 6
- doc_lengths: int32 [8, 8], P('dp'), may hold values from 1 to 4089, as said below
- cotangent: bfloat16 [8, 4096, 2048], P('dp', 'seq'), may hold values from -6 to 6
- ln1_gain: bfloat16 [2048], P(('dp', 'seq')), may hold values from 0.099609375 to 1.8984375
- ln1_bias: bfloat16 [2048], P(('dp', 'seq')), may hold values from -1.5 to 1.5
- w_qkv: bfloat16 [2048, 2304], P(('dp', 'seq')), may hold values from -0.125 to 0.125
- b_qv: bfloat16 [2176], P(('dp', 'seq')), may hold values from -2.5 to 2.5
- w_out: bfloat16 [2048, 2048], P(None, ('dp', 'seq')), may hold values from -1 to 1
- b_out: bfloat16 [2048], P(('dp', 'seq')), may hold values from -2.5 to 2.5
- ln2_gain: bfloat16 [2048], P(('dp', 'seq')), may hold values from 0.099609375 to 1.8984375
- ln2_bias: bfloat16 [2048], P(('dp', 'seq')), may hold values from -1.5 to 1.5
- w_up: bfloat16 [2048, 8192], P(('dp', 'seq')), may hold values from -0.125 to 0.125
- b_up: bfloat16 [8192], P(('dp', 'seq')), may hold values from -2.5 to 2.5
- w_down: bfloat16 [8192, 2048], P(('dp', 'seq')), may hold values from -0.0625 to 0.0625
- b_down: bfloat16 [2048], P(('dp', 'seq')), may hold values from -2.5 to 2.5
Outputs:
- mixed_out: bfloat16 [8, 4096, 2048], P('dp', 'seq')
- grad_hidden: float32 [8, 4096, 2048], P('dp', 'seq')
- grad_ln1_gain: float32 [2048], P(('dp', 'seq'))
- grad_ln1_bias: float32 [2048], P(('dp', 'seq'))
- grad_w_qkv: float32 [2048, 2304], P(('dp', 'seq'))
- grad_b_query: float32 [2048], P(('dp', 'seq'))
- grad_b_value: float32 [128], P(('dp', 'seq'))
- grad_w_out: float32 [2048, 2048], P(None, ('dp', 'seq'))
- grad_b_out: float32 [2048], P(('dp', 'seq'))
- grad_ln2_gain: float32 [2048], P(('dp', 'seq'))
- grad_ln2_bias: float32 [2048], P(('dp', 'seq'))
- grad_w_up: float32 [2048, 8192], P(('dp', 'seq'))
- grad_b_up: float32 [8192], P(('dp', 'seq'))
- grad_w_down: float32 [8192, 2048], P(('dp', 'seq'))
- grad_b_down: float32 [2048], P(('dp', 'seq'))
The draws below stay inside these ranges and needn't reach their ends.
Inputs may be any that keep to these rules, and one draw needn't show every extreme that they name: `doc_lengths`: the lengths of a window sum to at most 4096; the positions after its last document are padding. Some window holds a document of exactly 4089 tokens.
All inputs are finite; a program needn't handle non-finite values.
Results may differ from the reference program's by a relative error of at most 0.012.
Values may be sent and summed in bfloat16 or wider, within the bound.
No kernel may reach another device: no remote copies, remote signals or barrier semaphores. Data moves between devices by JAX's collectives and lax.ppermute only.
A program may use at most 448 MiB of HBM per device.

```python
import jax
import jax.numpy as jnp
from jax import lax

D = 2048
FF = 8192
HEADS = 16
HD = 128
LENGTH = 4096
DOCS = 8
WIN_DEV = 2
GROUP = 512
WINDOWS = 8


def draw_doc_lengths(key, part):
    key = jax.random.fold_in(key, 11)
    subkeys = jax.random.split(key, 6)
    doc_index = jnp.arange(DOCS, dtype=jnp.int32)[None, :]
    weights = jax.random.randint(subkeys[0], (WINDOWS, DOCS), 1, 17)
    pad_weight = jax.random.randint(subkeys[1], (WINDOWS, 1), 0, 2 * DOCS + 1)
    weight_sum = jnp.sum(weights, axis=1, keepdims=True) + pad_weight
    spread = jnp.maximum(weights * LENGTH // weight_sum, 1)
    short_most = max(1, GROUP // (2 * DOCS))
    short_docs = jax.random.randint(subkeys[2], (WINDOWS, DOCS), 1, short_most + 1)
    longest = jax.random.randint(subkeys[3], (WINDOWS, 1), 0, DOCS)
    chosen_slot = jax.random.randint(subkeys[5], (WINDOWS // WIN_DEV,), 0, WIN_DEV)
    window_index = jnp.arange(WINDOWS, dtype=jnp.int32)
    chosen = window_index % WIN_DEV == jnp.repeat(chosen_slot, WIN_DEV)
    extreme = (chosen & (window_index < WIN_DEV))[:, None]
    short_docs = jnp.where(extreme, 1, short_docs)
    short_docs = jnp.where(doc_index == (longest + 1) % DOCS, 1, short_docs)
    short_docs = jnp.where(doc_index == longest, 0, short_docs)
    padding = jax.random.randint(subkeys[4], (WINDOWS, 1), 0, GROUP // 2)
    padding = jnp.where(extreme, 0, padding)
    long_length = LENGTH - jnp.sum(short_docs, axis=1, keepdims=True) - padding
    spanning = jnp.where(doc_index == longest, long_length, short_docs)
    return jnp.where(chosen[:, None], spanning, spread).astype(jnp.int32)


def shard_levels(own_key, extent, shards, low, largest):
    loudness, own = 1.0, jax.random.fold_in(own_key, 6)
    for dim, blocks in shards:
        heights = jnp.exp(jax.random.uniform(jax.random.fold_in(own, dim), (blocks,), jnp.float32, low / len(shards), largest / len(shards)))
        loudness = loudness * jnp.repeat(heights, extent[dim] // blocks).reshape([-1 if axis == dim else 1 for axis in range(len(extent))])
    return loudness


def normal_values(rng, dims, deviation, limit, cuts=(), kind=jnp.bfloat16):
    entries = deviation * jax.random.normal(rng, dims, jnp.float32)
    if cuts:
        entries = entries * shard_levels(rng, dims, cuts, -0.22, 0.18)
    return jnp.clip(entries, -limit, limit).astype(kind)


def setup_inputs(seed: int = 0) -> dict:
    keys = jax.random.split(jax.random.key(seed), 16)
    hidden_in = normal_values(keys[0], (WINDOWS, LENGTH, D), 1.0, 6.0, ((0, 4), (1, 8)))
    doc_lengths = draw_doc_lengths(jax.random.fold_in(keys[15], 71), 0)
    cotangent = normal_values(keys[2], (WINDOWS, LENGTH, D), 1.0, 6.0, ((0, 4), (1, 8)))
    ln1_gain = jnp.clip(1.0 + 0.18 * jax.random.normal(keys[3], (D,), jnp.float32), 0.099609375, 1.8984375).astype(jnp.bfloat16)
    ln1_bias = normal_values(keys[4], (D,), 0.3, 1.5, ((0, 32),))
    w_qkv = normal_values(keys[5], (D, HEADS * HD + 2 * HD), D ** -0.5, 0.125, ((0, 32),))
    b_qv = normal_values(keys[6], (HEADS * HD + HD,), 0.5, 2.5, ((0, 32),))
    w_out = normal_values(keys[7], (HEADS * HD, D), (HEADS * HD // 64) ** -0.5, 1.0, ((1, 32),))
    b_out = normal_values(keys[8], (D,), 0.5, 2.5, ((0, 32),))
    ln2_gain = jnp.clip(1.0 + 0.18 * jax.random.normal(keys[9], (D,), jnp.float32), 0.099609375, 1.8984375).astype(jnp.bfloat16)
    ln2_bias = normal_values(keys[10], (D,), 0.3, 1.5, ((0, 32),))
    w_up = normal_values(keys[11], (D, FF), D ** -0.5, 0.125, ((0, 32),))
    b_up = normal_values(keys[12], (FF,), 0.5, 2.5, ((0, 32),))
    w_down = normal_values(keys[13], (FF, D), FF ** -0.5, 0.0625, ((0, 32),))
    b_down = normal_values(keys[14], (D,), 0.5, 2.5, ((0, 32),))
    return {"hidden_in": hidden_in, "doc_lengths": doc_lengths, "cotangent": cotangent, "ln1_gain": ln1_gain, "ln1_bias": ln1_bias, "w_qkv": w_qkv, "b_qv": b_qv, "w_out": w_out, "b_out": b_out, "ln2_gain": ln2_gain, "ln2_bias": ln2_bias, "w_up": w_up, "b_up": b_up, "w_down": w_down, "b_down": b_down}


@jax.custom_vjp
def low(v):
    return lax.optimization_barrier(v.astype(jnp.bfloat16)).astype(jnp.float32)

@jax.custom_vjp
def low_back(v):
    return v

def low_keep(v):
    return (low(v), None)

def low_pass(kept, grad):
    return (grad,)

def back_keep(v):
    return (v, None)

def back_low(kept, grad):
    return (low(grad),)
low.defvjp(low_keep, low_pass)
low_back.defvjp(back_keep, back_low)

def matmul(left_op, right_op):
    return jnp.dot(left_op, right_op, precision=lax.Precision.HIGHEST, preferred_element_type=jnp.float32)

def rounded_both(value_in):
    return low(low_back(value_in))

def layer_norm(values, gain_vec, offset):
    centre = lax.optimization_barrier(jnp.mean(values, axis=-1, keepdims=True))
    centred = values - centre
    spread = lax.optimization_barrier(jnp.mean(centred * centred, axis=-1, keepdims=True))
    return centred * lax.rsqrt(spread + 1e-05) * gain_vec + offset

def segment_ids(lengths):
    doc_ends = jnp.cumsum(lengths).astype(jnp.int32)
    position = jnp.arange(LENGTH, dtype=jnp.int32)
    return lax.optimization_barrier(jnp.sum((position[:, None] >= doc_ends[None, :]).astype(jnp.int32), axis=1)).astype(jnp.int32)

def window_forward(params, hidden, segments):
    ln1_gain, ln1_bias, w_qkv, b_qv, w_out, b_out, ln2_gain, ln2_bias, w_up, b_up, w_down, b_down = params
    width_q = HEADS * HD
    normed = low(layer_norm(hidden, ln1_gain, ln1_bias))
    projected = matmul(normed, w_qkv)
    queries = rounded_both(projected[:, :width_q] + b_qv[:width_q])
    keys_all = rounded_both(projected[:, width_q:width_q + HD])
    values_all = rounded_both(projected[:, width_q + HD:] + b_qv[width_q:])
    block_rows = min(512, LENGTH)
    block_count = LENGTH // block_rows
    position = jnp.arange(LENGTH, dtype=jnp.int32)
    scale_factor = HD ** (-0.5)

    def attend(pieces):
        query_block, query_pos, query_seg = pieces
        scores = jnp.einsum('qhd,kd->hqk', query_block, keys_all, precision=lax.Precision.HIGHEST) * scale_factor
        scores = low_back(scores)
        allowed = (query_pos[:, None] >= position[None, :]) & (query_seg[:, None] == segments[None, :])
        scores = jnp.where(allowed[None], scores, -1e+30)
        row_max = lax.optimization_barrier(jnp.max(scores, axis=-1, keepdims=True))
        exponent = jnp.exp(scores - row_max)
        softmax_rows = low(exponent / lax.optimization_barrier(jnp.sum(exponent, axis=-1, keepdims=True)))
        return jnp.einsum('hqk,kd->qhd', softmax_rows, values_all, precision=lax.Precision.HIGHEST)
    attended = lax.map(jax.checkpoint(attend), (queries.reshape(block_count, block_rows, HEADS, HD), position.reshape(block_count, block_rows), segments.reshape(block_count, block_rows)))
    attended = rounded_both(attended.reshape(LENGTH, width_q))
    residual = hidden + low_back(matmul(attended, w_out) + b_out)
    mixed_rows = low(layer_norm(residual, ln2_gain, ln2_bias))
    upward = low_back(matmul(mixed_rows, w_up) + b_up)
    active = low(jax.nn.gelu(upward, approximate=True))
    return residual + low_back(matmul(active, w_down) + b_down)

def reference(hidden_in, doc_lengths, cotangent, ln1_gain, ln1_bias, w_qkv, b_qv, w_out, b_out, ln2_gain, ln2_bias, w_up, b_up, w_down, b_down):
    params = tuple((weight.astype(jnp.float32) for weight in (ln1_gain, ln1_bias, w_qkv, b_qv, w_out, b_out, ln2_gain, ln2_bias, w_up, b_up, w_down, b_down)))

    def window_step(totals, window):
        hidden, lengths, upstream = window
        segments = segment_ids(lengths)
        valid_rows = (segments < DOCS).astype(jnp.float32)
        output, pullback = jax.vjp(lambda weights, inputs: window_forward(weights, inputs, segments), params, hidden.astype(jnp.float32))
        gradients, grad_hidden = pullback(upstream.astype(jnp.float32) * valid_rows[:, None])
        totals = jax.tree.map(lambda first, second: first + second, totals, gradients)
        return (totals, (output.astype(jnp.bfloat16), grad_hidden))
    zero_grads = tuple((jnp.zeros(weight.shape, jnp.float32) for weight in params))
    totals, (mixed_out, grad_hidden) = lax.scan(window_step, zero_grads, (hidden_in, doc_lengths, cotangent))
    width_q = HEADS * HD
    return (mixed_out, grad_hidden, totals[0], totals[1], totals[2], totals[3][:width_q], totals[3][width_q:], totals[4], totals[5], totals[6], totals[7], totals[8], totals[9], totals[10], totals[11])
```

```python
import functools

import jax
import jax.numpy as jnp
from jax import lax
from jax.experimental import pallas as pl
from jax.experimental.pallas import tpu as pltpu
from jax.sharding import Mesh
from jax.sharding import PartitionSpec as P

HEADS = 16
HD = 128
DOCS = 8
LOG2E = 1.4426950408889634
CHIPS = ("y", "x", "z")
EVERY = ("y", "x", "z", "core")
PAIR = [(0, 1), (1, 0)]
BF16 = jnp.bfloat16
F32 = jnp.float32


def key_place(j, tk, nums, w, i, chips_z, chip_len):
    first = j * tk
    owner = first // chip_len
    slot = lax.rem(nums[w, i, 5] - owner + chips_z, chips_z)
    return slot, pl.multiple_of(first - owner * chip_len, tk), first


def forward_kernel(tq, tk, heads, deps, nums, q_ref, k_ref, v_ref, start_ref, *refs):
    o_ref, lse_ref, acc, top, bias = refs[deps:]
    w, i = pl.program_id(0), pl.program_id(1)
    t0, lo, hi, full_lo, full_hi = (nums[w, i, n] for n in range(5))
    factor = HD**-0.5 * LOG2E
    acc[...] = jnp.zeros_like(acc)
    top[...] = jnp.full_like(top, -1e20)
    ones = jnp.ones((tk, HD), BF16)

    def tile(j, masked):
        slot, row, k0 = key_place(j, tk, nums, w, i, k_ref.shape[0], k_ref.shape[2])
        keys = k_ref[slot, 0, pl.ds(row, tk), :]
        values = jnp.concatenate([v_ref[slot, 0, pl.ds(row, tk), :], ones], axis=1)
        if masked:
            key_pos = k0 + lax.broadcasted_iota(jnp.int32, (tq, tk), 1)
            query_pos = t0 + lax.broadcasted_iota(jnp.int32, (tq, tk), 0)
            allowed = (key_pos <= query_pos) & (key_pos >= start_ref[...][:, :1])
            bias[...] = jnp.where(allowed, 0.0, -1e30)
        for h in range(heads):
            queries = q_ref[:, h * HD : (h + 1) * HD]
            scores = contract_cols(queries, keys) * factor
            if masked:
                scores = scores + bias[...]
            old = top[h]
            new = jnp.maximum(old, jnp.max(scores, axis=1, keepdims=True))
            probs = jnp.exp2(scores - jnp.concatenate([new] * (tk // HD), axis=1)).astype(BF16)
            fade = jnp.exp2(old - new)
            top[h] = new
            acc[h] = acc[h] * jnp.concatenate([fade, fade], axis=1) + plain_dot(probs, values)

    def step(j, carry):
        partial = (j < full_lo) | (j >= full_hi)

        @pl.when(partial)
        def _():
            tile(j, True)

        @pl.when(jnp.logical_not(partial))
        def _():
            tile(j, False)

        return carry

    lax.fori_loop(lo, hi, step, 0)
    lane = lax.broadcasted_iota(jnp.int32, (tq, HD), 1)
    stats = jnp.zeros((tq, HD), F32)
    for h in range(heads):
        total = acc[h, :, HD:]
        o_ref[:, h * HD : (h + 1) * HD] = (acc[h, :, :HD] / total).astype(BF16)
        stats = jnp.where(lane == h, top[h] + jnp.log2(total), stats)
    lse_ref[...] = jnp.transpose(stats)[:heads]


def attend_forward(queries, keys, values, starts, nums, tq, tk, deps=()):
    chips_z, windows, chip_len, _ = keys.shape
    rows, width = queries.shape
    heads = width // HD
    tiles = rows // windows // tq

    def block(w, i):
        return w * tiles + i

    spread = jnp.broadcast_to(starts.reshape(rows, 1), (rows, HD))
    key_spec = pl.BlockSpec((chips_z, 1, chip_len, HD), lambda w, i, n: (0, w, 0, 0))
    return pl.pallas_call(
        functools.partial(forward_kernel, tq, tk, heads, len(deps)),
        grid_spec=pltpu.PrefetchScalarGridSpec(
            num_scalar_prefetch=1,
            grid=(windows, tiles),
            in_specs=[
                pl.BlockSpec((tq, width), lambda w, i, n: (block(w, i), 0)),
                key_spec,
                key_spec,
                pl.BlockSpec((tq, HD), lambda w, i, n: (block(w, i), 0)),
            ]
            + [pl.BlockSpec(memory_space=pl.ANY)] * len(deps),
            out_specs=[
                pl.BlockSpec((tq, width), lambda w, i, n: (block(w, i), 0)),
                pl.BlockSpec((heads, tq), lambda w, i, n: (0, block(w, i))),
            ],
            scratch_shapes=[
                pltpu.VMEM((heads, tq, 2 * HD), F32),
                pltpu.VMEM((heads, tq, HD), F32),
                pltpu.VMEM((tq, tk), F32),
            ],
        ),
        out_shape=[
            jax.ShapeDtypeStruct((rows, width), BF16),
            jax.ShapeDtypeStruct((heads, rows), F32),
        ],
        compiler_params=pltpu.CompilerParams(vmem_limit_bytes=40 * 2**20),
        cost_estimate=pl.CostEstimate(
            flops=2 * rows * width * chip_len * chips_z, bytes_accessed=4 * rows * width,
            transcendentals=rows * heads * chip_len * chips_z // 4,
        ),
        name="attention_forward",
    )(nums, queries, keys, values, spread, *deps)


def backward_kernel(tq, tk, heads, deps, nums, q_ref, g_ref, o_ref, lse_ref, k_ref, v_ref, start_ref, *refs):
    (dq_ref, dk_ref, dv_ref, dq_acc, dk_acc, dv_acc, bias, delta, probs_all, grads_all, q_all, g_all, turned) = refs[deps:]
    w, i = pl.program_id(0), pl.program_id(1)
    t0, lo, hi, full_lo, full_hi = (nums[w, i, n] for n in range(5))
    scale = HD**-0.5
    factor = scale * LOG2E
    chips_z, chip_len = k_ref.shape[0], k_ref.shape[2]

    @pl.when(i == 0)
    def _():
        dk_acc[...] = jnp.zeros_like(dk_acc)
        dv_acc[...] = jnp.zeros_like(dv_acc)
        for s in range(chips_z):
            turned[s] = jnp.transpose(k_ref[s, 0])

    dq_acc[...] = jnp.zeros_like(dq_acc)
    ones = jnp.ones((8, HD), F32)
    for h in range(heads):
        cols = slice(h * HD, (h + 1) * HD)
        rows = slice(h * tq, (h + 1) * tq)
        product = g_ref[:, cols].astype(F32) * o_ref[:, cols].astype(F32)
        delta[h] = lax.dot_general(
            ones, product, (((1,), (1,)), ((), ())), precision=lax.Precision.HIGHEST, preferred_element_type=F32
        )
        q_all[rows, :] = q_ref[:, cols]
        g_all[rows, :] = g_ref[:, cols]

    def tile(j, masked):
        slot, row, k0 = key_place(j, tk, nums, w, i, chips_z, chip_len)
        keys = k_ref[slot, 0, pl.ds(row, tk), :]
        values = v_ref[slot, 0, pl.ds(row, tk), :]
        if masked:
            key_pos = k0 + lax.broadcasted_iota(jnp.int32, (tk, tq), 0)
            query_pos = t0 + lax.broadcasted_iota(jnp.int32, (tk, tq), 1)
            allowed = (key_pos <= query_pos) & (key_pos >= start_ref[:1, :])
            bias[...] = jnp.where(allowed, 0.0, -1e30)
        for h in range(heads):
            rows = slice(h * tq, (h + 1) * tq)
            scores = contract_cols(keys, q_all[rows, :]) * factor
            if masked:
                scores = scores + bias[...]
            probs = jnp.exp2(scores - lse_ref[h : h + 1, :])
            grad_probs = contract_cols(values, g_all[rows, :])
            probs_all[:, rows] = probs.astype(BF16)
            grads_all[:, rows] = (probs * (grad_probs - delta[h, :1, :])).astype(BF16)
        dk_acc[slot, pl.ds(row, tk), :] += plain_dot(grads_all[...], q_all[...])
        dv_acc[slot, pl.ds(row, tk), :] += plain_dot(probs_all[...], g_all[...])
        dq_acc[...] += plain_dot(turned[slot, :, pl.ds(row, tk)], grads_all[...])

    def step(j, carry):
        partial = (j < full_lo) | (j >= full_hi)

        @pl.when(partial)
        def _():
            tile(j, True)

        @pl.when(jnp.logical_not(partial))
        def _():
            tile(j, False)

        return carry

    lax.fori_loop(lo, hi, step, 0)
    for h in range(heads):
        rows = slice(h * tq, (h + 1) * tq)
        dq_ref[:, h * HD : (h + 1) * HD] = (jnp.transpose(dq_acc[:, rows]) * scale).astype(BF16)

    @pl.when(i == pl.num_programs(1) - 1)
    def _():
        dk_ref[:, 0] = (dk_acc[...] * scale).astype(BF16)
        dv_ref[:, 0] = dv_acc[...].astype(BF16)


def attend_backward(queries, grad_attended, first_row, attended, lse, keys, values, starts, nums, tq, tk, deps=()):
    chips_z, windows, chip_len, _ = keys.shape
    rows, width = queries.shape
    heads = width // HD
    tiles = rows // windows // tq
    skip = first_row // tq

    def block(w, i):
        return w * tiles + i

    spread = jnp.broadcast_to(starts.reshape(1, rows), (8, rows))
    row_spec = pl.BlockSpec((tq, width), lambda w, i, n: (block(w, i), 0))
    key_spec = pl.BlockSpec((chips_z, 1, chip_len, HD), lambda w, i, n: (0, w, 0, 0))
    key_shape = jax.ShapeDtypeStruct(keys.shape, BF16)
    return pl.pallas_call(
        functools.partial(backward_kernel, tq, tk, heads, len(deps)),
        grid_spec=pltpu.PrefetchScalarGridSpec(
            num_scalar_prefetch=1,
            grid=(windows, tiles),
            in_specs=[
                row_spec,
                pl.BlockSpec((tq, width), lambda w, i, n: (block(w, i) + skip, 0)),
                row_spec,
                pl.BlockSpec((heads, tq), lambda w, i, n: (0, block(w, i))),
                key_spec,
                key_spec,
                pl.BlockSpec((8, tq), lambda w, i, n: (0, block(w, i))),
            ]
            + [pl.BlockSpec(memory_space=pl.ANY)] * len(deps),
            out_specs=[row_spec, key_spec, key_spec],
            scratch_shapes=[
                pltpu.VMEM((HD, heads * tq), F32),
                pltpu.VMEM((chips_z, chip_len, HD), F32),
                pltpu.VMEM((chips_z, chip_len, HD), F32),
                pltpu.VMEM((tk, tq), F32),
                pltpu.VMEM((heads, 8, tq), F32),
                pltpu.VMEM((tk, heads * tq), BF16),
                pltpu.VMEM((tk, heads * tq), BF16),
                pltpu.VMEM((heads * tq, HD), BF16),
                pltpu.VMEM((heads * tq, HD), BF16),
                pltpu.VMEM((chips_z, HD, chip_len), BF16),
            ],
        ),
        out_shape=[jax.ShapeDtypeStruct((rows, width), BF16), key_shape, key_shape],
        compiler_params=pltpu.CompilerParams(vmem_limit_bytes=40 * 2**20),
        cost_estimate=pl.CostEstimate(
            flops=4 * rows * width * chip_len * chips_z, bytes_accessed=8 * rows * width,
            transcendentals=rows * heads * chip_len * chips_z // 4,
        ),
        name="attention_backward",
    )(nums, queries, grad_attended, attended, lse, keys, values, spread, *deps)


def tile_numbers(starts, positions, z, tq, tk):
    windows, local = starts.shape
    tiled = starts.reshape(windows, local // tq, tq)
    t0 = jnp.broadcast_to(positions.reshape(local // tq, tq)[None, :, 0], (windows, local // tq))
    first, last = tiled[:, :, 0], tiled[:, :, -1]
    return jnp.stack(
        [t0, first // tk, (t0 + tq - 1) // tk + 1, (last + tk - 1) // tk, (t0 + 1) // tk, jnp.broadcast_to(z, t0.shape)],
        axis=2,
    ).astype(jnp.int32)


def matmul_kernel(kind, chunk, n_extra, n_out, n_deps, finish, *refs):
    a_ref, b_ref = refs[0], refs[1]
    extras = refs[2:2+n_extra]
    outs = refs[2+n_extra+n_deps:2+n_extra+n_deps+n_out]
    scratch = refs[2+n_extra+n_deps+n_out:]
    if kind == "tn":
        turned = scratch[0]
        @pl.when(pl.program_id(1) == 0)
        def _():
            turned[...] = jnp.transpose(a_ref[...])
        left = turned
    else:
        left = a_ref
    rows = left.shape[0]
    for r in range(0, rows, chunk):
        part = pl.ds(r, chunk)
        if kind == "nt":
            total = lax.dot_general(left[part, :], b_ref[...], (((1,), (1,)), ((), ())), preferred_element_type=F32)
        else:
            total = jnp.dot(left[part, :], b_ref[...], preferred_element_type=F32)
        finish(part, total, extras, outs)


def store(part, total, extras, outs):
    outs[0][part, :] = total.astype(outs[0].dtype)


def matmul(kind, a, b, outs, finish=store, extras=(), tm=1024, tn=512, chunk=256, deps=(), a_rows=None, name="matmul"):
    if kind == "tn":
        k, m = a.shape; n = b.shape[1]
    elif kind == "nt":
        m, k = a.shape; n = b.shape[0]
    else:
        m, k = a.shape; n = b.shape[1]
    first = 0
    if a_rows is not None:
        first, m = a_rows
    tm = min(tm, m); tn = min(tn, n); chunk = min(chunk, tm)
    f0 = first // tm
    a_spec = pl.BlockSpec((k, tm), lambda i, j: (0, i)) if kind == "tn" else pl.BlockSpec((tm, k), lambda i, j: (i + f0, 0))
    b_spec = pl.BlockSpec((tn, k), lambda i, j: (j, 0)) if kind == "nt" else pl.BlockSpec((k, tn), lambda i, j: (0, j))
    tile = pl.BlockSpec((tm, tn), lambda i, j: (i, j))
    row = pl.BlockSpec((1, tn), lambda i, j: (0, j))
    spec = {"tile": tile, "row": row, "part": pl.BlockSpec((1, 8, tn), lambda i, j: (i, 0, j))}
    shape = {"tile": (m, n), "row": (1, n), "part": (m // tm, 8, n)}
    out_shape = [jax.ShapeDtypeStruct(shape[w], d) for d, w in outs]
    res = pl.pallas_call(
        functools.partial(matmul_kernel, kind, chunk, len(extras), len(outs), len(deps), finish),
        grid=(m // tm, n // tn),
        in_specs=[a_spec, b_spec] + [spec[w] for _, w in extras] + [pl.BlockSpec(memory_space=pl.ANY)] * len(deps),
        out_specs=[spec[w] for _, w in outs],
        scratch_shapes=[pltpu.VMEM((tm, k), BF16)] if kind == "tn" else [],
        out_shape=out_shape,
        compiler_params=pltpu.CompilerParams(vmem_limit_bytes=52 * 2**20),
        cost_estimate=pl.CostEstimate(flops=2*m*n*k, bytes_accessed=2*(m*k+n*k+m*n), transcendentals=0),
        name=name,
    )(a, b, *[e for e, _ in extras], *deps)
    return res[0] if len(outs) == 1 else res


def slope_finish(part, total, extras, outs):
    g = (total * extras[0][part, :].astype(F32)).astype(BF16)
    outs[0][part, :] = g
    sums = jnp.sum(g.astype(F32).reshape(-1, 8, g.shape[1]), axis=0)
    if part.start == 0:
        outs[1][0] = sums
    else:
        outs[1][0] += sums


def contract_rows(left_op, right_op):
    return lax.dot_general(left_op, right_op, (((0,), (0,)), ((), ())), preferred_element_type=F32)


def contract_cols(left_op, right_op):
    return lax.dot_general(left_op, right_op, (((1,), (1,)), ((), ())), preferred_element_type=F32)


def plain_dot(left_op, right_op):
    return jnp.dot(left_op, right_op, preferred_element_type=F32)


def normalise(values):
    centred = values - jnp.mean(values, axis=-1, keepdims=True)
    spread = jnp.mean(centred * centred, axis=-1, keepdims=True)
    inverse = lax.rsqrt(spread + 1e-05)
    return centred * inverse, inverse


def norm_backward(unit, inverse, gain, grad):
    scaled = grad * gain
    inner = jnp.mean(scaled * unit, axis=-1, keepdims=True)
    return (scaled - jnp.mean(scaled, axis=-1, keepdims=True) - unit * inner) * inverse


def gelu_parts(u):
    inner = 0.7978845608028654 * (u + 0.044715 * u * u * u)
    t = jnp.tanh(inner)
    slope = 0.5 * (1.0 + t) + 0.5 * u * (1.0 - t * t) * 0.7978845608028654 * (1.0 + 3 * 0.044715 * u * u)
    return 0.5 * u * (1.0 + t), slope


def swap(values, axis):
    return lax.ppermute(values, axis, PAIR)


def in_order(index, own, other):
    return jnp.where(index == 0, jnp.stack([own, other]), jnp.stack([other, own]))


def pick(values, index, axis):
    return lax.dynamic_index_in_dim(values, index, axis, keepdims=False)


def exchange_add(values, index, axis_name, dim):
    arrived = swap(pick(values, 1 - index, dim), axis_name)
    return pick(values, index, dim).astype(F32) + arrived.astype(F32)


def core_rows(core, first, second):
    own = jnp.where(core == 0, first, second)
    other = swap(jnp.where(core == 0, second, first), "core")
    return in_order(core, own, other).reshape(2 * own.shape[0], own.shape[1])


def place_kernel(steps, half, spot, *refs):
    pieces, out, held, arrive, leave = refs[: 4 * steps], *refs[4 * steps :]
    y, x, z = spot[0], spot[1], spot[2]
    moves = []
    for s in range(steps):
        from_z = lax.rem(z - s + steps, steps)
        for i in range(2):
            for k, to in enumerate(((i, x, 0), (i, 1 - x, 0), (y, i, 1), (1 - y, i, 1))):
                row = (((to[0] * 2 + to[1]) * steps + from_z) * 2 + to[2]) * half
                moves.append((4 * s + k, i, pl.multiple_of(row, half)))
    inward = [
        pltpu.make_async_copy(pieces[p].at[i], held.at[n], arrive.at[n]) for n, (p, i, _) in enumerate(moves)
    ]
    outward = [
        pltpu.make_async_copy(held.at[n], out.at[pl.ds(row, half), :], leave.at[n])
        for n, (_, _, row) in enumerate(moves)
    ]
    for copy in inward:
        copy.start()
    for n, copy in enumerate(inward):
        copy.wait()
        outward[n].start()
    for copy in outward:
        copy.wait()


def place(pieces, spot):
    steps = len(pieces) // 4
    _, half, cols = pieces[0].shape
    return pl.pallas_call(
        functools.partial(place_kernel, steps, half),
        grid_spec=pltpu.PrefetchScalarGridSpec(
            num_scalar_prefetch=1,
            grid=(1,),
            in_specs=[pl.BlockSpec(memory_space=pl.ANY)] * len(pieces),
            out_specs=pl.BlockSpec(memory_space=pl.ANY),
            scratch_shapes=[
                pltpu.VMEM((8 * steps, half, cols), BF16),
                pltpu.SemaphoreType.DMA((8 * steps,)),
                pltpu.SemaphoreType.DMA((8 * steps,)),
            ],
        ),
        out_shape=jax.ShapeDtypeStruct((8 * steps * half, cols), BF16),
        compiler_params=pltpu.CompilerParams(vmem_limit_bytes=32 * 2**20),
        name="place_weight",
    )(spot, *pieces)


def gather_pieces(block, y, x, chips_z):
    half = block.shape[0] // 2
    ring = [(i, (i + 1) % chips_z) for i in range(chips_z)]
    one, two = block[:half], block[half:]
    got_one, got_two = lax.ppermute(one, "y", PAIR), lax.ppermute(two, "x", PAIR)
    one, two = in_order(y, one, got_one), in_order(x, two, got_two)
    pieces = []
    for s in range(chips_z):
        last = s == chips_z - 1
        next_one = None if last else lax.ppermute(one, "z", ring)
        next_two = None if last else lax.ppermute(two, "z", ring)
        pieces += [one, lax.ppermute(one, "x", PAIR), two, lax.ppermute(two, "y", PAIR)]
        one, two = next_one, next_two
    return pieces


class Sum:
    def __init__(self, total, y, x, chips_z):
        self.cols = total.shape[1]
        self.half = total.shape[0] // (8 * chips_z)
        self.total, self.y, self.x, self.chips_z = total.reshape(2, 2, chips_z, 2, self.half, self.cols), y, x, chips_z
        self.sent = (self.cut(0, 1 - y, 0), self.cut(1, 1 - x, 1))

    def cut(self, dim, index, part):
        at, size = [0, 0, 0, part, 0, 0], [2, 2, self.chips_z, 1, self.half, self.cols]
        at[dim], size[dim] = index, 1
        return lax.dynamic_slice(self.total, at, size).reshape(2, self.chips_z, self.half, self.cols)

    def first(self):
        one, two = swap(self.sent[0], "y"), swap(self.sent[1], "x")
        self.one = (self.cut(0, self.y, 0).astype(F32) + one.astype(F32)).astype(BF16)
        self.two = (self.cut(1, self.x, 1).astype(F32) + two.astype(F32)).astype(BF16)
        self.sent = (pick(self.one, 1 - self.x, 0), pick(self.two, 1 - self.y, 0))

    def second(self):
        one, two = swap(self.sent[0], "x"), swap(self.sent[1], "y")
        one = (pick(self.one, self.x, 0).astype(F32) + one.astype(F32)).astype(BF16)
        two = (pick(self.two, self.y, 0).astype(F32) + two.astype(F32)).astype(BF16)
        self.both = jnp.stack([one, two], axis=1).reshape(-1, self.cols)

    def over_z(self):
        self.result = lax.psum_scatter(self.both, "z", scatter_dimension=0, tiled=True)
        return self.result.astype(F32)


def doubling(axis):
    size = lax.axis_size(axis)
    step = 1
    while step < size:
        yield step, [(i, i ^ step) for i in range(size)]
        step *= 2


def gather_small(vector):
    for axis in reversed(EVERY):
        index = lax.axis_index(axis)
        for step, pairs in doubling(axis):
            vector = in_order((index // step) % 2, vector, lax.ppermute(vector, axis, pairs))
    return vector.reshape(-1, vector.shape[-1])


def sum_small(vector):
    for axis in reversed(EVERY):
        for _, pairs in doubling(axis):
            vector = vector + lax.ppermute(vector, axis, pairs)
    return vector


def own_rows(core, rows):
    pair = rows.reshape(2, rows.shape[0] // 2, rows.shape[1])
    own = pick(pair, core, 0)
    other = swap(pick(pair, 1 - core, 0), "core")
    return in_order(core, own, other)


def body(
    hidden_in, doc_lengths, cotangent, ln1_gain, ln1_bias, w_qkv, b_qv, w_out, b_out,
    ln2_gain, ln2_bias, w_up, b_up, w_down, b_down,
):
    windows, local_len, width = hidden_in.shape
    own_count = windows * local_len
    count = 2 * own_count
    chips_z = lax.axis_size("z")
    chips = 2 * lax.axis_size("y") * chips_z
    y, x, z, core = (lax.axis_index(name) for name in EVERY)
    width_q = HEADS * HD
    half_q = width_q // 2
    chip_len = 2 * local_len
    length = chip_len * chips_z
    hidden_units = w_up.shape[1]
    unit_block = hidden_units // (2 * chips)

    doc_ends = jnp.cumsum(doc_lengths, axis=1)
    cores = jnp.stack([core, 1 - core])
    positions = (z * chip_len + cores[:, None] * local_len + jnp.arange(local_len, dtype=jnp.int32)[None, :]).astype(jnp.int32)
    ended = positions[:, None, :, None] >= doc_ends[None, :, None, :]
    starts = jnp.max(jnp.where(ended, doc_ends[None, :, None, :], 0), axis=3)
    valid = (jnp.sum(ended[0].astype(jnp.int32), axis=2) < DOCS).reshape(own_count, 1)

    vectors = (ln1_gain, ln1_bias, b_qv, b_out, ln2_gain, ln2_bias, b_up, b_down)
    sizes = [v.shape[0] for v in vectors]
    packed = gather_small(jnp.concatenate(vectors)).astype(F32)
    full = []
    at = 0
    for size in sizes:
        full.append(packed[:, at : at + size].reshape(-1))
        at += size
    gain1, bias1, bias_qv, bias_out, gain2, bias2, bias_up, bias_down = full
    bias_up = pick(bias_up.reshape(chips, 2, unit_block), core, 1).reshape(-1)
    bias_qkv = jnp.where(
        core == 0,
        jnp.concatenate([bias_qv[:half_q], jnp.zeros((HD,), F32)]),
        jnp.concatenate([bias_qv[half_q:width_q], bias_qv[width_q:]]),
    )
    qkv_block = core_rows(
        core,
        jnp.concatenate([w_qkv[:, :half_q], w_qkv[:, width_q : width_q + HD]], axis=1),
        jnp.concatenate([w_qkv[:, half_q:width_q], w_qkv[:, width_q + HD :]], axis=1),
    )
    w_out_t = w_out.T
    out_block = core_rows(core, w_out_t[:, :half_q], w_out_t[:, half_q:])
    up_parts = w_up.reshape(w_up.shape[0], chips, 2, unit_block)
    up_block = core_rows(
        core,
        up_parts[:, :, 0].reshape(w_up.shape[0], -1),
        up_parts[:, :, 1].reshape(w_up.shape[0], -1),
    )
    spot = jnp.stack([y, x, z]).astype(jnp.int32)
    by_hand = lax.axis_size("y") == 2

    def gather(block):
        return lax.all_gather(block, CHIPS, axis=0, tiled=True)

    if by_hand:
        w_qkv_all = place(gather_pieces(qkv_block, y, x, chips_z), spot)
        w_out_all = place(gather_pieces(out_block, y, x, chips_z), spot)
    else:
        w_qkv_all, w_out_all = gather(qkv_block), gather(out_block)
    w_up_all, w_down_all = gather(up_block), gather(w_down)

    tokens = hidden_in.reshape(own_count, width).astype(F32)
    unit1, inverse1 = normalise(tokens)
    normed1_own = (unit1 * gain1 + bias1).astype(BF16)
    normed1 = jnp.concatenate([normed1_own, swap(normed1_own, "core")], axis=0)
    own_kv = (plain_dot(normed1, w_qkv_all[:, half_q:]) + bias_qkv[half_q:]).astype(BF16)
    own_kv = own_kv.reshape(2, windows, local_len, HD)
    own_kv = jnp.swapaxes(in_order(core, own_kv[0], own_kv[1]), 0, 1).reshape(windows, chip_len, HD)
    ring = [(i, (i + 1) % chips_z) for i in range(chips_z)]
    keys, values = [], []
    for s in range(chips_z):
        other_kv = swap(own_kv, "core")
        keys.append(jnp.where(core == 0, own_kv, other_kv))
        values.append(jnp.where(core == 0, other_kv, own_kv))
        if s < chips_z - 1:
            own_kv = lax.ppermute(own_kv, "z", ring)
    keys, values = jnp.stack(keys), jnp.stack(values)
    projected = (plain_dot(normed1, w_qkv_all[:, :half_q]) + bias_qkv[:half_q]).astype(BF16)
    queries = (projected[:own_count], projected[own_count:])
    tq_forward, tk_forward = min(512, local_len), min(512, chip_len)
    tq, tk = min(256, local_len), min(256, chip_len)
    attended, lse = [None, None], [None, None]
    for n in (1, 0):
        attended[n], lse[n] = attend_forward(
            queries[n], keys, values, starts[n],
            tile_numbers(starts[n], positions[n], z, tq_forward, tk_forward), tq_forward, tk_forward,
        )
        if n == 1:
            out_other = swap(plain_dot(attended[1], w_out_all.T).astype(BF16), "core")
    residual = tokens + bias_out + plain_dot(attended[0], w_out_all.T) + out_other.astype(F32)
    attended_all = jnp.concatenate(attended, axis=0)

    unit2, inverse2 = normalise(residual)
    normed2_own = (unit2 * gain2 + bias2).astype(BF16)
    normed2 = jnp.concatenate([normed2_own, swap(normed2_own, "core")], axis=0)
    upward = plain_dot(normed2, w_up_all) + bias_up
    active, slope = gelu_parts(upward)
    active = active.astype(BF16)
    upstream = jnp.where(valid, cotangent.reshape(own_count, width), 0)
    grad_down = jnp.concatenate([upstream, swap(upstream, "core")], axis=0)
    grad_b_down = jnp.sum(upstream.astype(F32), axis=0)
    down_total = contract_rows(active, grad_down).astype(BF16)

    if by_hand:
        down_sum = Sum(down_total, y, x, chips_z)
    grad_up, unit_sums = matmul(
        "nt", grad_down, w_down_all, [(BF16, "tile"), (F32, "part")], slope_finish, [(slope, "tile")],
        deps=down_sum.sent if by_hand else (), name="grad_up",
    )
    grad_b_up = jnp.sum(unit_sums, axis=(0, 1))
    up_total = matmul("tn", normed2, grad_up, [(BF16, "tile")], name="grad_w_up")
    if by_hand:
        down_sum.first()
        up_sum = Sum(up_total, y, x, chips_z)
    grad_other = matmul(
        "nt", grad_up, w_up_all, [(BF16, "tile")], a_rows=(own_count, own_count),
        deps=down_sum.sent + up_sum.sent if by_hand else (), name="grad_normed2",
    )
    grad_mixed = contract_cols(grad_up[:own_count], w_up_all) + swap(grad_other, "core").astype(F32)
    grad_gain2 = jnp.sum(grad_mixed * unit2, axis=0)
    grad_bias2 = jnp.sum(grad_mixed, axis=0)
    grad_residual = upstream.astype(F32) + norm_backward(unit2, inverse2, gain2, grad_mixed)
    branch_own = grad_residual.astype(BF16)
    grad_b_out = jnp.sum(branch_own.astype(F32), axis=0)
    branch = jnp.concatenate([branch_own, swap(branch_own, "core")], axis=0)
    if by_hand:
        down_sum.second()
        grad_w_down = down_sum.over_z()
    down_other = matmul(
        "nn", active, w_down_all, [(BF16, "tile")], a_rows=(own_count, own_count),
        deps=(branch_own, down_sum.both) if by_hand else (branch_own,), name="mixed_out",
    )
    mixed_out = (
        residual + bias_down + plain_dot(active[:own_count], w_down_all) + swap(down_other, "core").astype(F32)
    ).astype(BF16)
    if by_hand:
        up_sum.first()

    grad_attended = matmul(
        "nn", branch, w_out_all, [(BF16, "tile")], deps=up_sum.sent if by_hand else (), name="grad_attended"
    )
    out_total = matmul("tn", branch, attended_all, [(BF16, "tile")], name="grad_w_out")
    if by_hand:
        out_sum = Sum(out_total, y, x, chips_z)
        up_sum.second()
        grad_w_up = up_sum.over_z()
    grad_query, grad_keys, grad_values = [None, None], [None, None], [None, None]
    for n in (0, 1):
        deps = ()
        if by_hand:
            if n == 0:
                deps = out_sum.sent + (up_sum.both, mixed_out)
            else:
                out_sum.first()
                deps = out_sum.sent + (grad_keys[0], down_sum.result)
        grad_query[n], grad_keys[n], grad_values[n] = attend_backward(
            queries[n], grad_attended, n * own_count, attended[n], lse[n], keys, values, starts[n],
            tile_numbers(starts[n], positions[n], z, tq, tk), tq, tk, deps,
        )
    grad_keys = grad_keys[0].astype(F32) + grad_keys[1].astype(F32)
    grad_values = grad_values[0].astype(F32) + grad_values[1].astype(F32)
    arrived = swap(jnp.where(core == 0, grad_values, grad_keys).astype(BF16), "core")
    grad_kv = (jnp.where(core == 0, grad_keys, grad_values) + arrived.astype(F32)).astype(BF16)
    running = grad_kv[1 % chips_z]
    for s in range(2, chips_z + 1):
        running = (grad_kv[s % chips_z].astype(F32) + lax.ppermute(running, "z", ring).astype(F32)).astype(BF16)
    grad_kv = jnp.swapaxes(running.reshape(windows, 2, local_len, HD), 0, 1)
    grad_kv = in_order(core, grad_kv[0], grad_kv[1]).reshape(count, HD)
    grad_qkv = jnp.concatenate([jnp.concatenate(grad_query, axis=0), grad_kv], axis=1)
    grad_b_qkv = jnp.sum(grad_qkv.astype(F32), axis=0)
    qkv_total = contract_rows(normed1, grad_qkv).astype(BF16)
    grad_other = contract_cols(grad_qkv[own_count:], w_qkv_all).astype(BF16)
    grad_normed = contract_cols(grad_qkv[:own_count], w_qkv_all) + swap(grad_other, "core").astype(F32)
    grad_gain1 = jnp.sum(grad_normed * unit1, axis=0)
    grad_bias1 = jnp.sum(grad_normed, axis=0)
    grad_hidden = grad_residual + norm_backward(unit1, inverse1, gain1, grad_normed)

    if by_hand:
        qkv_sum = Sum(qkv_total, y, x, chips_z)
        out_sum.second()
        grad_w_out = out_sum.over_z()
        qkv_sum.first()
        qkv_sum.second()
        grad_w_qkv = qkv_sum.over_z()
    else:
        grad_w_down, grad_w_up, grad_w_out, grad_w_qkv = (
            lax.psum_scatter(total, CHIPS, scatter_dimension=0, tiled=True).astype(F32)
            for total in (down_total, up_total, out_total, qkv_total)
        )
    zero = jnp.zeros_like(grad_b_qkv[:half_q])
    query_bias = jnp.where(
        core == 0, jnp.concatenate([grad_b_qkv[:half_q], zero]), jnp.concatenate([zero, grad_b_qkv[:half_q]])
    )
    value_bias = jnp.where(core == 0, 0.0, grad_b_qkv[half_q:])
    unit_bias = in_order(core, grad_b_up.reshape(chips, unit_block), jnp.zeros((chips, unit_block), F32))
    unit_bias = jnp.swapaxes(unit_bias, 0, 1).reshape(-1)
    device = ((y * 2 + x) * chips_z + z) * 2 + core
    mine = []
    for group in ((grad_b_out, grad_gain2, grad_bias2, unit_bias, grad_b_down), (grad_gain1, grad_bias1, query_bias, value_bias)):
        sums = sum_small(jnp.concatenate(group))
        at = 0
        for part in group:
            size = part.shape[0] // (2 * chips)
            mine.append(lax.dynamic_slice_in_dim(sums, at + device * size, size, 0))
            at += part.shape[0]
    own_qkv = own_rows(core, grad_w_qkv)
    own_qkv = jnp.concatenate(
        [own_qkv[0, :, :half_q], own_qkv[1, :, :half_q], own_qkv[0, :, half_q:], own_qkv[1, :, half_q:]], axis=1
    )
    own_out = own_rows(core, grad_w_out)
    own_out = jnp.concatenate([own_out[0], own_out[1]], axis=1).T
    own_up = own_rows(core, grad_w_up)
    own_up = jnp.moveaxis(own_up.reshape(2, own_up.shape[1], chips, unit_block), 0, 2).reshape(own_up.shape[1], -1)
    return (
        mixed_out.reshape(windows, local_len, width),
        grad_hidden.reshape(windows, local_len, width),
        mine[5], mine[6], own_qkv, mine[7], mine[8], own_out, mine[0], mine[1], mine[2],
        own_up, mine[3], grad_w_down, mine[4],
    )


def solution(mesh):
    split = Mesh(mesh.devices.reshape(mesh.shape["dp"] // 2, 2, mesh.shape["seq"] // 2, 2), EVERY)
    rows = ("y", "x")
    cols = ("z", "core")
    vector, matrix = P(EVERY), P(EVERY, None)
    tokens = P(rows, cols, None)
    return jax.shard_map(
        body,
        mesh=split,
        in_specs=(
            tokens, P(rows, None), tokens, vector, vector, matrix, vector, P(None, EVERY), vector,
            vector, vector, matrix, vector, matrix, vector,
        ),
        out_specs=(
            tokens, tokens, vector, vector, matrix, vector, vector, P(None, EVERY), vector, vector, vector,
            matrix, vector, matrix, vector,
        ),
        check_vma=False,
    )
```

```python
import functools

import jax
import jax.numpy as jnp
from jax import lax
from jax.experimental import pallas as pl
from jax.experimental.pallas import tpu as pltpu
from jax.sharding import Mesh
from jax.sharding import PartitionSpec as P

HEADS = 16
HD = 128
DOCS = 8
LOG2E = 1.4426950408889634
CHIPS = ("y", "x", "z")
EVERY = ("y", "x", "z", "core")
PAIR = [(0, 1), (1, 0)]
BF16 = jnp.bfloat16
F32 = jnp.float32


def key_place(j, tk, nums, w, i, chips_z, chip_len):
    first = j * tk
    owner = first // chip_len
    slot = lax.rem(nums[w, i, 5] - owner + chips_z, chips_z)
    return slot, pl.multiple_of(first - owner * chip_len, tk), first


def forward_kernel(tq, tk, heads, deps, nums, q_ref, k_ref, v_ref, start_ref, *refs):
    o_ref, lse_ref, acc, top, bias = refs[deps:]
    w, i = pl.program_id(0), pl.program_id(1)
    t0, lo, hi, full_lo, full_hi = (nums[w, i, n] for n in range(5))
    factor = HD**-0.5 * LOG2E
    acc[...] = jnp.zeros_like(acc)
    top[...] = jnp.full_like(top, -1e20)
    ones = jnp.ones((tk, HD), BF16)

    def tile(j, masked):
        slot, row, k0 = key_place(j, tk, nums, w, i, k_ref.shape[0], k_ref.shape[2])
        keys = k_ref[slot, 0, pl.ds(row, tk), :]
        values = jnp.concatenate([v_ref[slot, 0, pl.ds(row, tk), :], ones], axis=1)
        if masked:
            key_pos = k0 + lax.broadcasted_iota(jnp.int32, (tq, tk), 1)
            query_pos = t0 + lax.broadcasted_iota(jnp.int32, (tq, tk), 0)
            allowed = (key_pos <= query_pos) & (key_pos >= start_ref[...][:, :1])
            bias[...] = jnp.where(allowed, 0.0, -1e30)
        for h in range(heads):
            queries = q_ref[:, h * HD : (h + 1) * HD]
            scores = contract_cols(queries, keys) * factor
            if masked:
                scores = scores + bias[...]
            old = top[h]
            new = jnp.maximum(old, jnp.max(scores, axis=1, keepdims=True))
            probs = jnp.exp2(scores - jnp.concatenate([new] * (tk // HD), axis=1)).astype(BF16)
            fade = jnp.exp2(old - new)
            top[h] = new
            acc[h] = acc[h] * jnp.concatenate([fade, fade], axis=1) + plain_dot(probs, values)

    def step(j, carry):
        partial = (j < full_lo) | (j >= full_hi)

        @pl.when(partial)
        def _():
            tile(j, True)

        @pl.when(jnp.logical_not(partial))
        def _():
            tile(j, False)

        return carry

    lax.fori_loop(lo, hi, step, 0)
    lane = lax.broadcasted_iota(jnp.int32, (tq, HD), 1)
    stats = jnp.zeros((tq, HD), F32)
    for h in range(heads):
        total = acc[h, :, HD:]
        o_ref[:, h * HD : (h + 1) * HD] = (acc[h, :, :HD] / total).astype(BF16)
        stats = jnp.where(lane == h, top[h] + jnp.log2(total), stats)
    lse_ref[...] = jnp.transpose(stats)[:heads]


def attend_forward(queries, keys, values, starts, nums, tq, tk, deps=()):
    chips_z, windows, chip_len, _ = keys.shape
    rows, width = queries.shape
    heads = width // HD
    tiles = rows // windows // tq

    def block(w, i):
        return w * tiles + i

    spread = jnp.broadcast_to(starts.reshape(rows, 1), (rows, HD))
    key_spec = pl.BlockSpec((chips_z, 1, chip_len, HD), lambda w, i, n: (0, w, 0, 0))
    return pl.pallas_call(
        functools.partial(forward_kernel, tq, tk, heads, len(deps)),
        grid_spec=pltpu.PrefetchScalarGridSpec(
            num_scalar_prefetch=1,
            grid=(windows, tiles),
            in_specs=[
                pl.BlockSpec((tq, width), lambda w, i, n: (block(w, i), 0)),
                key_spec,
                key_spec,
                pl.BlockSpec((tq, HD), lambda w, i, n: (block(w, i), 0)),
            ]
            + [pl.BlockSpec(memory_space=pl.ANY)] * len(deps),
            out_specs=[
                pl.BlockSpec((tq, width), lambda w, i, n: (block(w, i), 0)),
                pl.BlockSpec((heads, tq), lambda w, i, n: (0, block(w, i))),
            ],
            scratch_shapes=[
                pltpu.VMEM((heads, tq, 2 * HD), F32),
                pltpu.VMEM((heads, tq, HD), F32),
                pltpu.VMEM((tq, tk), F32),
            ],
        ),
        out_shape=[
            jax.ShapeDtypeStruct((rows, width), BF16),
            jax.ShapeDtypeStruct((heads, rows), F32),
        ],
        compiler_params=pltpu.CompilerParams(vmem_limit_bytes=40 * 2**20),
        cost_estimate=pl.CostEstimate(
            flops=2 * rows * width * chip_len * chips_z, bytes_accessed=4 * rows * width,
            transcendentals=rows * heads * chip_len * chips_z // 4,
        ),
        name="attention_forward",
    )(nums, queries, keys, values, spread, *deps)


def backward_kernel(tq, tk, heads, deps, nums, q_ref, g_ref, o_ref, lse_ref, k_ref, v_ref, start_ref, *refs):
    (dq_ref, dk_ref, dv_ref, dq_acc, dk_acc, dv_acc, bias, delta, probs_all, grads_all, q_all, g_all, turned) = refs[deps:]
    w, i = pl.program_id(0), pl.program_id(1)
    t0, lo, hi, full_lo, full_hi = (nums[w, i, n] for n in range(5))
    scale = HD**-0.5
    factor = scale * LOG2E
    chips_z, chip_len = k_ref.shape[0], k_ref.shape[2]

    @pl.when(i == 0)
    def _():
        dk_acc[...] = jnp.zeros_like(dk_acc)
        dv_acc[...] = jnp.zeros_like(dv_acc)
        for s in range(chips_z):
            turned[s] = jnp.transpose(k_ref[s, 0])

    dq_acc[...] = jnp.zeros_like(dq_acc)
    ones = jnp.ones((8, HD), F32)
    for h in range(heads):
        cols = slice(h * HD, (h + 1) * HD)
        rows = slice(h * tq, (h + 1) * tq)
        product = g_ref[:, cols].astype(F32) * o_ref[:, cols].astype(F32)
        delta[h] = lax.dot_general(
            ones, product, (((1,), (1,)), ((), ())), precision=lax.Precision.HIGHEST, preferred_element_type=F32
        )
        q_all[rows, :] = q_ref[:, cols]
        g_all[rows, :] = g_ref[:, cols]

    def tile(j, masked):
        slot, row, k0 = key_place(j, tk, nums, w, i, chips_z, chip_len)
        keys = k_ref[slot, 0, pl.ds(row, tk), :]
        values = v_ref[slot, 0, pl.ds(row, tk), :]
        if masked:
            key_pos = k0 + lax.broadcasted_iota(jnp.int32, (tk, tq), 0)
            query_pos = t0 + lax.broadcasted_iota(jnp.int32, (tk, tq), 1)
            allowed = (key_pos <= query_pos) & (key_pos >= start_ref[:1, :])
            bias[...] = jnp.where(allowed, 0.0, -1e30)
        for h in range(heads):
            rows = slice(h * tq, (h + 1) * tq)
            scores = contract_cols(keys, q_all[rows, :]) * factor
            if masked:
                scores = scores + bias[...]
            probs = jnp.exp2(scores - lse_ref[h : h + 1, :])
            grad_probs = contract_cols(values, g_all[rows, :])
            probs_all[:, rows] = probs.astype(BF16)
            grads_all[:, rows] = (probs * (grad_probs - delta[h, :1, :])).astype(BF16)
        dk_acc[slot, pl.ds(row, tk), :] += plain_dot(grads_all[...], q_all[...])
        dv_acc[slot, pl.ds(row, tk), :] += plain_dot(probs_all[...], g_all[...])
        dq_acc[...] += plain_dot(turned[slot, :, pl.ds(row, tk)], grads_all[...])

    def step(j, carry):
        partial = (j < full_lo) | (j >= full_hi)

        @pl.when(partial)
        def _():
            tile(j, True)

        @pl.when(jnp.logical_not(partial))
        def _():
            tile(j, False)

        return carry

    lax.fori_loop(lo, hi, step, 0)
    for h in range(heads):
        rows = slice(h * tq, (h + 1) * tq)
        dq_ref[:, h * HD : (h + 1) * HD] = (jnp.transpose(dq_acc[:, rows]) * scale).astype(BF16)

    @pl.when(i == pl.num_programs(1) - 1)
    def _():
        dk_ref[:, 0] = (dk_acc[...] * scale).astype(BF16)
        dv_ref[:, 0] = dv_acc[...].astype(BF16)


def attend_backward(queries, grad_attended, first_row, attended, lse, keys, values, starts, nums, tq, tk, deps=()):
    chips_z, windows, chip_len, _ = keys.shape
    rows, width = queries.shape
    heads = width // HD
    tiles = rows // windows // tq
    skip = first_row // tq

    def block(w, i):
        return w * tiles + i

    spread = jnp.broadcast_to(starts.reshape(1, rows), (8, rows))
    row_spec = pl.BlockSpec((tq, width), lambda w, i, n: (block(w, i), 0))
    key_spec = pl.BlockSpec((chips_z, 1, chip_len, HD), lambda w, i, n: (0, w, 0, 0))
    key_shape = jax.ShapeDtypeStruct(keys.shape, BF16)
    return pl.pallas_call(
        functools.partial(backward_kernel, tq, tk, heads, len(deps)),
        grid_spec=pltpu.PrefetchScalarGridSpec(
            num_scalar_prefetch=1,
            grid=(windows, tiles),
            in_specs=[
                row_spec,
                pl.BlockSpec((tq, width), lambda w, i, n: (block(w, i) + skip, 0)),
                row_spec,
                pl.BlockSpec((heads, tq), lambda w, i, n: (0, block(w, i))),
                key_spec,
                key_spec,
                pl.BlockSpec((8, tq), lambda w, i, n: (0, block(w, i))),
            ]
            + [pl.BlockSpec(memory_space=pl.ANY)] * len(deps),
            out_specs=[row_spec, key_spec, key_spec],
            scratch_shapes=[
                pltpu.VMEM((HD, heads * tq), F32),
                pltpu.VMEM((chips_z, chip_len, HD), F32),
                pltpu.VMEM((chips_z, chip_len, HD), F32),
                pltpu.VMEM((tk, tq), F32),
                pltpu.VMEM((heads, 8, tq), F32),
                pltpu.VMEM((tk, heads * tq), BF16),
                pltpu.VMEM((tk, heads * tq), BF16),
                pltpu.VMEM((heads * tq, HD), BF16),
                pltpu.VMEM((heads * tq, HD), BF16),
                pltpu.VMEM((chips_z, HD, chip_len), BF16),
            ],
        ),
        out_shape=[jax.ShapeDtypeStruct((rows, width), BF16), key_shape, key_shape],
        compiler_params=pltpu.CompilerParams(vmem_limit_bytes=40 * 2**20),
        cost_estimate=pl.CostEstimate(
            flops=4 * rows * width * chip_len * chips_z, bytes_accessed=8 * rows * width,
            transcendentals=rows * heads * chip_len * chips_z // 4,
        ),
        name="attention_backward",
    )(nums, queries, grad_attended, attended, lse, keys, values, spread, *deps)


def tile_numbers(starts, positions, z, tq, tk):
    windows, local = starts.shape
    tiled = starts.reshape(windows, local // tq, tq)
    t0 = jnp.broadcast_to(positions.reshape(local // tq, tq)[None, :, 0], (windows, local // tq))
    first, last = tiled[:, :, 0], tiled[:, :, -1]
    return jnp.stack(
        [t0, first // tk, (t0 + tq - 1) // tk + 1, (last + tk - 1) // tk, (t0 + 1) // tk, jnp.broadcast_to(z, t0.shape)],
        axis=2,
    ).astype(jnp.int32)


def store(part, total, extras, outs):
    outs[0][part, :] = total.astype(outs[0].dtype)


def sum_finish(part, total, extras, outs):
    total = total + extras[0][part, :] + extras[1][...] + extras[2][part, :].astype(F32)
    outs[0][part, :] = total.astype(BF16)


def slope_finish(part, total, extras, outs):
    grad = (total * extras[0][part, :].astype(F32)).astype(BF16)
    outs[0][part, :] = grad
    sums = jnp.sum(grad.astype(F32).reshape(-1, 8, grad.shape[1]), axis=0)
    if part.start == 0:
        outs[1][...] = sums
    else:
        outs[1][...] += sums


def gelu_finish(part, total, extras, outs):
    u = total + extras[0][...]
    square = u * u
    s = 0.5 * jnp.tanh(u * (0.7978845608028654 + (0.7978845608028654 * 0.044715) * square)) + 0.5
    value = u * s
    outs[0][part, :] = value.astype(BF16)
    rate = 2 * 0.7978845608028654 + (6 * 0.7978845608028654 * 0.044715) * square
    outs[1][part, :] = (s + value * (1.0 - s) * rate).astype(BF16)


def rows_kernel(kind, chunk, extra_count, dep_count, finish, a_ref, b_ref, *refs):
    extras, outs = refs[:extra_count], refs[extra_count + dep_count :]
    dot = contract_cols if kind == "nt" else plain_dot
    for r in range(0, a_ref.shape[0], chunk):
        part = pl.ds(r, chunk)
        finish(part, dot(a_ref[part, :], b_ref[...]), extras, outs)


def matmul(kind, a, b, outs, finish=store, extras=(), tn=512, chunk=256, deps=(), name="matmul"):
    m, k = a.shape
    n = b.shape[0] if kind == "nt" else b.shape[1]
    tn, chunk = min(tn, n), min(chunk, m)
    tile = pl.BlockSpec((m, tn), lambda j: (0, j))
    spec = {
        "tile": tile,
        "row": pl.BlockSpec((1, tn), lambda j: (0, j)),
        "sums": pl.BlockSpec((8, tn), lambda j: (0, j)),
    }
    shape = {"tile": (m, n), "sums": (8, n)}
    res = pl.pallas_call(
        functools.partial(rows_kernel, kind, chunk, len(extras), len(deps), finish),
        grid=(n // tn,),
        in_specs=[
            pl.BlockSpec((m, k), lambda j: (0, 0)),
            pl.BlockSpec((tn, k), lambda j: (j, 0)) if kind == "nt" else pl.BlockSpec((k, tn), lambda j: (0, j)),
        ]
        + [spec[kind_of] for _, kind_of in extras]
        + [pl.BlockSpec(memory_space=pl.ANY)] * len(deps),
        out_specs=[spec[w] for _, w in outs],
        out_shape=[jax.ShapeDtypeStruct(shape[w], d) for d, w in outs],
        compiler_params=pltpu.CompilerParams(vmem_limit_bytes=52 * 2**20),
        cost_estimate=pl.CostEstimate(flops=2 * m * n * k, bytes_accessed=2 * (m * k + n * k + m * n), transcendentals=0),
        name=name,
    )(a, b, *[array for array, _ in extras], *deps)
    return res[0] if len(outs) == 1 else res


def tokens_kernel(chunk, dep_count, a0_ref, a1_ref, b0_ref, b1_ref, *refs):
    out, left = refs[dep_count:]

    @pl.when(pl.program_id(1) == 0)
    def _():
        left[0] = jnp.transpose(a0_ref[...])
        left[1] = jnp.transpose(a1_ref[...])

    for r in range(0, left.shape[1], chunk):
        part = pl.ds(r, chunk)
        out[part, :] = (plain_dot(left[0, part, :], b0_ref[...]) + plain_dot(left[1, part, :], b1_ref[...])).astype(BF16)


def over_tokens(a, b, tm=2048, tn=512, chunk=256, deps=(), b_cols=None, name="weight_gradient"):
    k, m = a[0].shape
    first, n = b_cols or (0, b[0].shape[1])
    tm, tn, chunk = min(tm, m), min(tn, n), min(chunk, m)
    skip = first // tn
    a_spec = pl.BlockSpec((k, tm), lambda i, j: (0, i))
    b_spec = pl.BlockSpec((k, tn), lambda i, j: (0, j + skip))
    return pl.pallas_call(
        functools.partial(tokens_kernel, chunk, len(deps)),
        grid=(m // tm, n // tn),
        in_specs=[a_spec, a_spec, b_spec, b_spec] + [pl.BlockSpec(memory_space=pl.ANY)] * len(deps),
        out_specs=pl.BlockSpec((tm, tn), lambda i, j: (i, j)),
        scratch_shapes=[pltpu.VMEM((2, tm, k), BF16)],
        out_shape=jax.ShapeDtypeStruct((m, n), BF16),
        compiler_params=pltpu.CompilerParams(vmem_limit_bytes=52 * 2**20),
        cost_estimate=pl.CostEstimate(flops=4 * m * n * k, bytes_accessed=4 * (m * k + n * k + m * n), transcendentals=0),
        name=name,
    )(*a, *b, *deps)


def contract_rows(left_op, right_op):
    return lax.dot_general(left_op, right_op, (((0,), (0,)), ((), ())), preferred_element_type=F32)


def contract_cols(left_op, right_op):
    return lax.dot_general(left_op, right_op, (((1,), (1,)), ((), ())), preferred_element_type=F32)


def plain_dot(left_op, right_op):
    return jnp.dot(left_op, right_op, preferred_element_type=F32)


def normalise(values):
    centred = values - jnp.mean(values, axis=-1, keepdims=True)
    spread = jnp.mean(centred * centred, axis=-1, keepdims=True)
    inverse = lax.rsqrt(spread + 1e-05)
    return centred * inverse, inverse


def norm_kernel(rounded, dep_count, own_ref, got_ref, unit_ref, inverse_ref, gain_ref, base_ref, *refs):
    outs = refs[dep_count:]
    grad = own_ref[...] + got_ref[...].astype(F32)
    unit = unit_ref[...]
    scaled = grad * gain_ref[...]
    inner = jnp.mean(scaled * unit, axis=-1, keepdims=True)
    level = jnp.mean(scaled, axis=-1, keepdims=True)
    result = base_ref[...].astype(F32) + (scaled - level - unit * inner) * inverse_ref[...][:, :1]
    outs[0][...] = result
    terms = [grad * unit, grad]
    if rounded:
        low = result.astype(BF16)
        outs[3][...] = low
        terms.append(low.astype(F32))
    first = pl.program_id(0) == 0
    for term, out in zip(terms, (outs[1], outs[2], outs[-1])):
        sums = jnp.sum(term.reshape(-1, 8, term.shape[1]), axis=0)

        @pl.when(first)
        def _(out=out, sums=sums):
            out[...] = sums

        @pl.when(jnp.logical_not(first))
        def _(out=out, sums=sums):
            out[...] += sums


def norm_backward(own, got, unit, inverse, gain, base, rounded, deps=()):
    rows, cols = own.shape
    tile = min(128, rows)
    block = pl.BlockSpec((tile, cols), lambda i: (i, 0))
    sums = pl.BlockSpec((8, cols), lambda i: (0, 0))
    sums_shape = jax.ShapeDtypeStruct((8, cols), F32)
    out_specs, out_shape = [block, sums, sums], [jax.ShapeDtypeStruct((rows, cols), F32), sums_shape, sums_shape]
    if rounded:
        out_specs += [block, sums]
        out_shape += [jax.ShapeDtypeStruct((rows, cols), BF16), sums_shape]
    return pl.pallas_call(
        functools.partial(norm_kernel, rounded, len(deps)),
        grid=(rows // tile,),
        in_specs=[
            block, block, block, pl.BlockSpec((tile, HD), lambda i: (i, 0)), pl.BlockSpec((1, cols), lambda i: (0, 0)), block,
        ]
        + [pl.BlockSpec(memory_space=pl.ANY)] * len(deps),
        out_specs=out_specs,
        out_shape=out_shape,
        compiler_params=pltpu.CompilerParams(vmem_limit_bytes=40 * 2**20),
        name="norm_backward",
    )(own, got, unit, jnp.broadcast_to(inverse, (rows, HD)), gain.reshape(1, cols), base, *deps)


def swap(values, axis):
    return lax.ppermute(values, axis, PAIR)


def in_order(index, own, other):
    return jnp.where(index == 0, jnp.stack([own, other]), jnp.stack([other, own]))


def pick(values, index, axis):
    return lax.dynamic_index_in_dim(values, index, axis, keepdims=False)


def exchange_add(values, index, axis_name, dim):
    arrived = swap(pick(values, 1 - index, dim), axis_name)
    return pick(values, index, dim).astype(F32) + arrived.astype(F32)


def core_rows(core, first, second):
    own = jnp.where(core == 0, first, second)
    other = swap(jnp.where(core == 0, second, first), "core")
    return in_order(core, own, other).reshape(2 * own.shape[0], own.shape[1])


def hold_kernel(dep_count, value_ref, *refs):
    refs[dep_count][...] = value_ref[...]


def hold(value, *deps):
    whole = pl.BlockSpec(value.shape, lambda: (0,) * value.ndim)
    return pl.pallas_call(
        functools.partial(hold_kernel, len(deps)),
        in_specs=[whole] + [pl.BlockSpec(memory_space=pl.ANY)] * len(deps),
        out_specs=whole,
        out_shape=jax.ShapeDtypeStruct(value.shape, value.dtype),
        name="hold",
    )(value, *deps)


def place_kernel(moves_of, whole_count, half, dep_count, spot, *refs):
    count = len(moves_of)
    pieces = refs[:count]
    whole = refs[count : count + whole_count]
    out, held, arrive, leave = refs[count + whole_count + dep_count :]
    y, x, z = spot[0], spot[1], spot[2]
    steps = count // 4
    parts = 2 + whole_count * 2
    moves = []
    for n, move in enumerate(moves_of):
        s, k = move
        from_z = lax.rem(z - s + steps, steps)
        for i in range(2):
            to = ((i, x, 0), (i, 1 - x, 0), (y, i, 1), (1 - y, i, 1))[k]
            row = (((to[0] * 2 + to[1]) * steps + from_z) * parts + whole_count * 2 + to[2]) * half
            moves.append((pieces[n].at[i], pl.multiple_of(row, half), half))
    for array in whole:
        for chip in range(4 * steps):
            moves.append((array.at[pl.ds(chip * 2 * half, 2 * half), :], chip * parts * half, 2 * half))
    inward, outward, at = [], [], 0
    for n, (source, row, rows) in enumerate(moves):
        here = held.at[pl.ds(at, rows), :]
        inward.append(pltpu.make_async_copy(source, here, arrive.at[n]))
        outward.append(pltpu.make_async_copy(here, out.at[pl.ds(row, rows), :], leave.at[n]))
        at += rows
    for copy in inward:
        copy.start()
    for n, copy in enumerate(inward):
        copy.wait()
        outward[n].start()
    for copy in outward:
        copy.wait()


def place(pieces, spot, whole=(), deps=()):
    steps = len(pieces) // 4
    _, half, cols = pieces[0].shape
    count = 8 * steps + 4 * steps * len(whole)
    rows = 8 * steps * half * (1 + len(whole))
    moves_of = [(s, k) for s in range(steps) for k in range(4)]
    return pl.pallas_call(
        functools.partial(place_kernel, moves_of, len(whole), half, len(deps)),
        grid_spec=pltpu.PrefetchScalarGridSpec(
            num_scalar_prefetch=1,
            grid=(1,),
            in_specs=[pl.BlockSpec(memory_space=pl.ANY)] * (len(pieces) + len(whole) + len(deps)),
            out_specs=pl.BlockSpec(memory_space=pl.ANY),
            scratch_shapes=[
                pltpu.VMEM((rows, cols), BF16),
                pltpu.SemaphoreType.DMA((count,)),
                pltpu.SemaphoreType.DMA((count,)),
            ],
        ),
        out_shape=jax.ShapeDtypeStruct((rows, cols), BF16),
        compiler_params=pltpu.CompilerParams(vmem_limit_bytes=32 * 2**20),
        name="place_weight",
    )(spot, *pieces, *whole, *deps)


def gather_pieces(block, y, x, chips_z):
    half = block.shape[0] // 2
    ring = [(i, (i + 1) % chips_z) for i in range(chips_z)]
    one, two = block[:half], block[half:]
    got_one, got_two = swap(one, "y"), swap(two, "x")
    one, two = in_order(y, one, got_one), in_order(x, two, got_two)
    pieces, stages = [], []
    for s in range(chips_z):
        stages.append((one, two))
        pieces += [one, swap(one, "x"), two, swap(two, "y")]
        if s < chips_z - 1:
            one, two = lax.ppermute(one, "z", ring), lax.ppermute(two, "z", ring)
    return pieces, stages


def fold_kernel(spot, own_one, own_two, got_one, got_two, *refs):
    keep_one, send_one, keep_two, send_two = refs[-4:]
    y, x = spot[0], spot[1]
    for mine, own, got, keep, send in ((x, own_one, got_one, keep_one, send_one), (y, own_two, got_two, keep_two, send_two)):
        for index, out in ((mine, keep), (1 - mine, send)):
            total = own[own_at(own, index)].astype(F32) + got[index, 0].astype(F32)
            out[0] = total.astype(BF16)


def own_at(ref, index):
    return (index, 0, 0, 0) if ref.shape[0] == 2 else (0, index, 0, 0)


def fold_again_kernel(count, *refs):
    out = refs[-1]
    cols = out.shape[-1] // count
    for n in range(count):
        keep_one, keep_two, got_one, got_two = refs[4 * n : 4 * n + 4]
        here = pl.ds(n * cols, cols)
        out[0, 0, :, here] = (keep_one[0].astype(F32) + got_one[0].astype(F32)).astype(BF16)
        out[0, 1, :, here] = (keep_two[0].astype(F32) + got_two[0].astype(F32)).astype(BF16)


class Sum:
    def __init__(self, total, spot, chips_z):
        self.cols = total.shape[1]
        self.half = total.shape[0] // (8 * chips_z)
        self.total, self.spot, self.chips_z = total.reshape(2, 2, chips_z, 2, self.half, self.cols), spot, chips_z
        self.sent = (self.cut(0, 1 - spot[0], 0), self.cut(1, 1 - spot[1], 1))

    def cut(self, dim, index, part):
        at, size = [0, 0, 0, part, 0, 0], [2, 2, self.chips_z, 1, self.half, self.cols]
        at[dim], size[dim] = index, 1
        return lax.dynamic_slice(self.total, at, size).reshape(2, self.chips_z, self.half, self.cols)

    def first(self, *deps):
        got = (swap(self.sent[0], "y"), swap(self.sent[1], "x"))
        block = (self.half, self.cols)
        got_spec = pl.BlockSpec((2, 1, *block), lambda z, spot: (0, z, 0, 0))
        out_spec = pl.BlockSpec((1, *block), lambda z, spot: (z, 0, 0))
        keep_one, send_one, keep_two, send_two = pl.pallas_call(
            fold_kernel,
            grid_spec=pltpu.PrefetchScalarGridSpec(
                num_scalar_prefetch=1,
                grid=(self.chips_z,),
                in_specs=[
                    pl.BlockSpec((1, 2, 1, 1, *block), lambda z, spot: (spot[0], 0, z, 0, 0, 0)),
                    pl.BlockSpec((2, 1, 1, 1, *block), lambda z, spot: (0, spot[1], z, 1, 0, 0)),
                    got_spec,
                    got_spec,
                ]
                + [pl.BlockSpec(memory_space=pl.ANY)] * len(deps),
                out_specs=[out_spec] * 4,
            ),
            out_shape=[jax.ShapeDtypeStruct((self.chips_z, *block), BF16)] * 4,
            compiler_params=pltpu.CompilerParams(vmem_limit_bytes=32 * 2**20),
            name="fold",
        )(self.spot, self.total, self.total, *got, *deps)
        self.keep, self.sent = (keep_one, keep_two), (send_one, send_two)

    def second(self, *deps, beside=()):
        sums = (self, *beside)
        arrays = []
        for one in sums:
            arrays += [*one.keep, swap(one.sent[0], "x"), swap(one.sent[1], "y")]
        self.cols *= len(sums)
        self.both = pl.pallas_call(
            functools.partial(fold_again_kernel, len(sums)),
            grid=(self.chips_z,),
            in_specs=[pl.BlockSpec((1, *array.shape[1:]), lambda z: (z, 0, 0)) for array in arrays]
            + [pl.BlockSpec(memory_space=pl.ANY)] * len(deps),
            out_specs=pl.BlockSpec((1, 2, self.half, self.cols), lambda z: (z, 0, 0, 0)),
            out_shape=jax.ShapeDtypeStruct((self.chips_z, 2, self.half, self.cols), BF16),
            compiler_params=pltpu.CompilerParams(vmem_limit_bytes=32 * 2**20),
            name="fold_again",
        )(*arrays, *deps).reshape(-1, self.cols)

    def round_z(self, ring):
        z = self.spot[2]
        both = self.both.reshape(self.chips_z, -1, self.cols)
        running = pick(both, (z + self.chips_z - 1) % self.chips_z, 0)
        for s in range(2, self.chips_z + 1):
            mine = pick(both, (z + self.chips_z - s) % self.chips_z, 0)
            total = mine.astype(F32) + lax.ppermute(running, "z", ring).astype(F32)
            running = total.astype(BF16)
        return total

    def over_z(self):
        self.result = lax.psum_scatter(self.both, "z", scatter_dimension=0, tiled=True)
        return self.result.astype(F32)


def pack_kernel(spot, gain1, bias1, query0, query1, out_bias, gain2, bias2, up0, up1, down_bias, packed):
    width = packed.shape[1]
    core = spot[0]
    packed[...] = jnp.zeros_like(packed)
    for n, ref in enumerate((gain1, bias1, out_bias, gain2, bias2, down_bias)):
        packed[n : n + 1, :] = jnp.sum(ref[...], axis=0, keepdims=True)
    units = jnp.sum(up0[...] + up1[...], axis=0, keepdims=True)
    count = units.shape[1] // width
    for n in range(count):
        packed[pl.ds(8 + core * count + n, 1), :] = units[:, n * width : (n + 1) * width]
    columns = jnp.sum(query0[...], axis=0, keepdims=True) + jnp.sum(query1[...], axis=0, keepdims=True)
    half = width // 2
    for n in range(2):
        packed[6:7, n * half : (n + 1) * half] = jnp.where(core == n, columns[:, :half], 0.0)
    packed[7:8, :HD] = jnp.where(core == 0, 0.0, columns[:, half:])


def pack(core, *arrays):
    width = arrays[0].shape[1]
    units = arrays[7].shape[1] // width
    return pl.pallas_call(
        pack_kernel,
        grid_spec=pltpu.PrefetchScalarGridSpec(
            num_scalar_prefetch=1,
            grid=(1,),
            in_specs=[pl.BlockSpec(a.shape, lambda i, spot: (0, 0)) for a in arrays],
            out_specs=pl.BlockSpec((8 + 2 * units, width), lambda i, spot: (0, 0)),
        ),
        out_shape=jax.ShapeDtypeStruct((8 + 2 * units, width), F32),
        compiler_params=pltpu.CompilerParams(vmem_limit_bytes=32 * 2**20),
        name="pack_small",
    )(core.reshape(1).astype(jnp.int32), *arrays)


def doubling(axis):
    size = lax.axis_size(axis)
    step = 1
    while step < size:
        yield step, [(i, i ^ step) for i in range(size)]
        step *= 2


def gather_small(vector):
    for axis in reversed(EVERY):
        index = lax.axis_index(axis)
        for step, pairs in doubling(axis):
            vector = in_order((index // step) % 2, vector, lax.ppermute(vector, axis, pairs))
    return vector.reshape(-1, vector.shape[-1])


def sum_small(vector):
    for axis in reversed(EVERY):
        for _, pairs in doubling(axis):
            vector = vector + lax.ppermute(vector, axis, pairs)
    return vector


def join_kernel(cut, core, own, other, out):
    cols = own.shape[1]
    rest = cols - cut
    for n in range(2):
        for index, ref in ((n, own), (1 - n, other)):

            @pl.when(core[0] == n)
            def _(index=index, ref=ref):
                out[:, index * cut : (index + 1) * cut] = ref[:, :cut]
                out[:, 2 * cut + index * rest : 2 * cut + (index + 1) * rest] = ref[:, cut:]


def join_columns(core, own, other, cut):
    rows, cols = own.shape
    whole = pl.BlockSpec((rows, cols), lambda i, spot: (0, 0))
    return pl.pallas_call(
        functools.partial(join_kernel, cut),
        grid_spec=pltpu.PrefetchScalarGridSpec(
            num_scalar_prefetch=1,
            grid=(1,),
            in_specs=[whole, whole],
            out_specs=pl.BlockSpec((rows, 2 * cols), lambda i, spot: (0, 0)),
        ),
        out_shape=jax.ShapeDtypeStruct((rows, 2 * cols), F32),
        name="join_columns",
    )(core.reshape(1).astype(jnp.int32), own, other)


def own_rows(core, rows):
    pair = rows.reshape(2, rows.shape[0] // 2, rows.shape[1])
    own = pick(pair, core, 0)
    other = swap(pick(pair, 1 - core, 0), "core")
    return in_order(core, own, other)


def body(
    hidden_in, doc_lengths, cotangent, ln1_gain, ln1_bias, w_qkv, b_qv, w_out, b_out,
    ln2_gain, ln2_bias, w_up, b_up, w_down, b_down,
):
    windows, local_len, width = hidden_in.shape
    own_count = windows * local_len
    count = 2 * own_count
    chips_z = lax.axis_size("z")
    chips = 2 * lax.axis_size("y") * chips_z
    y, x, z, core = (lax.axis_index(name) for name in EVERY)
    width_q = HEADS * HD
    half_q = width_q // 2
    chip_len = 2 * local_len
    length = chip_len * chips_z
    hidden_units = w_up.shape[1]
    unit_block = hidden_units // (2 * chips)

    doc_ends = jnp.cumsum(doc_lengths, axis=1)
    cores = jnp.stack([core, 1 - core])
    positions = (z * chip_len + cores[:, None] * local_len + jnp.arange(local_len, dtype=jnp.int32)[None, :]).astype(jnp.int32)
    ended = positions[:, None, :, None] >= doc_ends[None, :, None, :]
    starts = jnp.max(jnp.where(ended, doc_ends[None, :, None, :], 0), axis=3)
    valid = (jnp.sum(ended[0].astype(jnp.int32), axis=2) < DOCS).reshape(own_count, 1)

    vectors = (ln1_gain, ln1_bias, b_qv, b_out, ln2_gain, ln2_bias, b_up, b_down)
    sizes = [v.shape[0] for v in vectors]
    packed = gather_small(jnp.concatenate(vectors)).astype(F32)
    full = []
    at = 0
    for size in sizes:
        full.append(packed[:, at : at + size].reshape(-1))
        at += size
    gain1, bias1, bias_qv, bias_out, gain2, bias2, bias_up, bias_down = full
    bias_up = pick(bias_up.reshape(chips, 2, unit_block), core, 1).reshape(-1)
    bias_qkv = jnp.where(
        core == 0,
        jnp.concatenate([bias_qv[:half_q], jnp.zeros((HD,), F32)]),
        jnp.concatenate([bias_qv[half_q:width_q], bias_qv[width_q:]]),
    )
    w_out_t = w_out.T
    near_block = core_rows(
        core,
        jnp.concatenate([w_qkv[:, :half_q], w_qkv[:, width_q : width_q + HD], w_out_t[:, :half_q]], axis=1),
        jnp.concatenate([w_qkv[:, half_q:width_q], w_qkv[:, width_q + HD :], w_out_t[:, half_q:]], axis=1),
    )
    up_parts = w_up.reshape(w_up.shape[0], chips, 2, unit_block)
    up_block = core_rows(
        core,
        up_parts[:, :, 0].reshape(w_up.shape[0], -1),
        up_parts[:, :, 1].reshape(w_up.shape[0], -1),
    )
    spot = jnp.stack([y, x, z]).astype(jnp.int32)
    by_hand = lax.axis_size("y") == 2
    ring = [(i, (i + 1) % chips_z) for i in range(chips_z)]

    def gather(block):
        return lax.all_gather(block, CHIPS, axis=0, tiled=True)

    def both_cores(own):
        return (own, swap(own, "core"))

    near_all, w_up_all = gather(near_block), gather(up_block)
    w_out_all = near_all[:, half_q + HD :]

    tokens = hidden_in.reshape(own_count, width).astype(F32)
    unit1, inverse1 = normalise(tokens)
    normed1 = both_cores((unit1 * gain1 + bias1).astype(BF16))
    w_query, w_kv = near_all[:, :half_q], near_all[:, half_q : half_q + HD]
    own_kv = [(plain_dot(rows, w_kv) + bias_qkv[half_q:]).astype(BF16) for rows in normed1]
    own_kv = [rows.reshape(windows, local_len, HD) for rows in own_kv]
    own_kv = jnp.swapaxes(in_order(core, *own_kv), 0, 1).reshape(windows, chip_len, HD)
    keys, values = [], []
    for s in range(chips_z):
        other_kv = swap(own_kv, "core")
        keys.append(jnp.where(core == 0, own_kv, other_kv))
        values.append(jnp.where(core == 0, other_kv, own_kv))
        if s < chips_z - 1:
            own_kv = lax.ppermute(own_kv, "z", ring)
    w_down_all = gather(w_down)
    keys, values = jnp.stack(keys), jnp.stack(values)
    queries = [(plain_dot(rows, w_query) + bias_qkv[:half_q]).astype(BF16) for rows in normed1]
    tq_forward, tk_forward = min(512, local_len), min(512, chip_len)
    tq, tk = min(256, local_len), min(256, chip_len)
    attended, lse = [None, None], [None, None]
    for n in (1, 0):
        attended[n], lse[n] = attend_forward(
            queries[n], keys, values, starts[n],
            tile_numbers(starts[n], positions[n], z, tq_forward, tk_forward), tq_forward, tk_forward,
            () if n == 1 else (attended[1],),
        )
        if n == 1:
            out_other = swap(matmul("nt", attended[1], w_out_all, [(BF16, "tile")], name="attention_out"), "core")
    residual = tokens + bias_out + contract_cols(attended[0], w_out_all) + out_other.astype(F32)

    unit2, inverse2 = normalise(residual)
    normed2 = both_cores((unit2 * gain2 + bias2).astype(BF16))
    active, slope = [None, None], [None, None]
    for n in (0, 1):
        active[n], slope[n] = matmul(
            "nn", normed2[n], w_up_all, [(BF16, "tile"), (BF16, "tile")], gelu_finish, [(bias_up.reshape(1, -1), "row")],
            name="upward",
        )
    upstream = jnp.where(valid, cotangent.reshape(own_count, width), 0)
    grad_down = both_cores(upstream)
    down_total = over_tokens(active, grad_down, name="grad_w_down")

    deps = ()
    if by_hand:
        down_sum = Sum(down_total, spot, chips_z)
        deps = down_sum.sent
    grad_up, unit_sums = [None, None], [None, None]
    for n in (0, 1):
        grad_up[n], unit_sums[n] = matmul(
            "nt", grad_down[n], w_down_all, [(BF16, "tile"), (F32, "sums")], slope_finish, [(slope[n], "tile")],
            deps=deps, name="grad_up",
        )
    cols = grad_up[0].shape[1] // 2
    up_totals = [over_tokens(normed2, grad_up, b_cols=(n * cols, cols), name="grad_w_up") for n in (0, 1)]
    if by_hand:
        down_sum.first(up_totals[1])
        up_sums = [Sum(total, spot, chips_z) for total in up_totals]
        deps = down_sum.sent + up_sums[0].sent + up_sums[1].sent
    mixed_other = matmul("nt", grad_up[1], w_up_all, [(BF16, "tile")], deps=deps, name="grad_normed2")
    mixed_own = matmul("nt", grad_up[0], w_up_all, [(F32, "tile")], deps=(mixed_other,), name="grad_normed2")
    down_other = matmul("nn", active[1], w_down_all, [(BF16, "tile")], deps=(mixed_own,), name="mixed_out")
    deps = (down_other,)
    if by_hand:
        down_sum.second(down_other)
        up_sums[0].first(down_other)
        grad_w_down = down_sum.over_z()
        deps += (down_sum.both,) + up_sums[0].sent
    grad_residual, gain2_sums, bias2_sums, branch_own, out_sums = norm_backward(
        mixed_own, swap(mixed_other, "core"), unit2, inverse2, gain2, upstream, True, deps
    )
    branch = both_cores(branch_own)

    grad_attended = [matmul("nn", branch[n], w_out_all, [(BF16, "tile")], name="grad_attended") for n in (0, 1)]
    out_total = over_tokens(branch, attended, deps=(grad_attended[1],), name="grad_w_out")
    if by_hand:
        out_sum = Sum(out_total, spot, chips_z)
        up_sums[1].first(out_total)
    grad_query, grad_keys, grad_values = [None, None], [None, None], [None, None]
    for n in (0, 1):
        deps = ()
        if by_hand:
            if n == 0:
                deps = out_sum.sent + up_sums[1].sent
            else:
                up_sums[0].second(grad_keys[0], beside=up_sums[1:])
                grad_w_up = up_sums[0].over_z()
                deps = (up_sums[0].both, down_sum.result)
        grad_query[n], grad_keys[n], grad_values[n] = attend_backward(
            queries[n], grad_attended[n], 0, attended[n], lse[n], keys, values, starts[n],
            tile_numbers(starts[n], positions[n], z, tq, tk), tq, tk, deps,
        )
    if by_hand:
        out_sum.first(grad_keys[1])
    grad_keys = grad_keys[0].astype(F32) + grad_keys[1].astype(F32)
    grad_values = grad_values[0].astype(F32) + grad_values[1].astype(F32)
    kv_sent = jnp.where(core == 0, grad_values, grad_keys).astype(BF16)
    query_total = over_tokens(
        normed1, grad_query, deps=(kv_sent,), name="grad_w_query"
    )
    grad_kv = (jnp.where(core == 0, grad_keys, grad_values) + swap(kv_sent, "core").astype(F32)).astype(BF16)
    running = hold(grad_kv[1 % chips_z], query_total, *((up_sums[0].result,) if by_hand else ()))
    for s in range(2, chips_z + 1):
        running = (grad_kv[s % chips_z].astype(F32) + lax.ppermute(running, "z", ring).astype(F32)).astype(BF16)
    grad_kv = jnp.swapaxes(running.reshape(windows, 2, local_len, HD), 0, 1)
    grad_kv = in_order(core, grad_kv[0], grad_kv[1]).reshape(2, own_count, HD)
    kv_total = (contract_rows(normed1[0], grad_kv[0]) + contract_rows(normed1[1], grad_kv[1])).astype(BF16)
    qkv_total = jnp.concatenate([query_total, kv_total], axis=1)
    mixed_out = matmul(
        "nn", active[0], w_down_all, [(BF16, "tile")], sum_finish,
        [(residual, "tile"), (bias_down.reshape(1, -1), "row"), (swap(down_other, "core"), "tile")], deps=(query_total,), name="mixed_out",
    )
    grad_qkv = [jnp.concatenate([grad_query[n], grad_kv[n]], axis=1) for n in (0, 1)]
    deps = (mixed_out,)
    if by_hand:
        out_sum.second(mixed_out)
        grad_w_out = out_sum.over_z()
        qkv_sum = Sum(qkv_total, spot, chips_z)
        deps += qkv_sum.sent + (out_sum.both,)
    first_other = matmul("nt", grad_qkv[1], near_all, [(BF16, "tile")], deps=deps, name="grad_normed1")
    first_own = matmul("nt", grad_qkv[0], near_all, [(F32, "tile")], deps=(first_other,), name="grad_normed1")
    grad_hidden, gain1_sums, bias1_sums = norm_backward(
        first_own, swap(first_other, "core"), unit1, inverse1, gain1, grad_residual, False
    )
    if by_hand:
        qkv_sum.first(gain1_sums)
        qkv_sum.second()
        grad_w_qkv = qkv_sum.round_z(ring)
    qkv_sums = [jnp.sum(rows.astype(F32).reshape(-1, 8, rows.shape[1]), axis=0) for rows in grad_qkv]
    down_sums = jnp.sum(upstream.astype(F32).reshape(-1, 8, width), axis=0)

    if not by_hand:
        grad_w_down, grad_w_up, grad_w_out, grad_w_qkv = (
            lax.psum_scatter(total, CHIPS, scatter_dimension=0, tiled=True).astype(F32)
            for total in (down_total, jnp.concatenate(up_totals, axis=1), out_total, qkv_total)
        )
    device = ((y * 2 + x) * chips_z + z) * 2 + core
    share = width // (2 * chips)
    sums = sum_small(
        pack(
            core, gain1_sums, bias1_sums, *qkv_sums, out_sums, gain2_sums, bias2_sums, *unit_sums, down_sums,
        )
    )
    vectors = lax.dynamic_slice(sums, (0, device * share), (7, share))
    value_bias = lax.dynamic_slice(sums, (7, device * (HD // (2 * chips))), (1, HD // (2 * chips)))[0]
    unit_bias = lax.dynamic_slice_in_dim(
        sums[8:].reshape(2, -1), ((y * 2 + x) * chips_z + z) * unit_block, unit_block, 1
    )
    unit_bias = pick(unit_bias, core, 0)
    pair = grad_w_qkv.reshape(2, -1, half_q + HD)
    own_qkv = join_columns(core, pick(pair, core, 0), swap(pick(pair, 1 - core, 0), "core"), half_q)
    own_out = own_rows(core, grad_w_out)
    own_out = jnp.concatenate([own_out[0], own_out[1]], axis=1).T
    own_up = own_rows(core, grad_w_up)
    own_up = jnp.moveaxis(own_up.reshape(2, own_up.shape[1], chips, unit_block), 0, 2).reshape(own_up.shape[1], -1)
    return (
        mixed_out.reshape(windows, local_len, width),
        grad_hidden.reshape(windows, local_len, width),
        vectors[0], vectors[1], own_qkv, vectors[6], value_bias, own_out, vectors[2], vectors[3], vectors[4],
        own_up, unit_bias, grad_w_down, vectors[5],
    )


def solution(mesh):
    split = Mesh(mesh.devices.reshape(mesh.shape["dp"] // 2, 2, mesh.shape["seq"] // 2, 2), EVERY)
    rows = ("y", "x")
    cols = ("z", "core")
    vector, matrix = P(EVERY), P(EVERY, None)
    tokens = P(rows, cols, None)
    return jax.shard_map(
        body,
        mesh=split,
        in_specs=(
            tokens, P(rows, None), tokens, vector, vector, matrix, vector, P(None, EVERY), vector,
            vector, vector, matrix, vector, matrix, vector,
        ),
        out_specs=(
            tokens, tokens, vector, vector, matrix, vector, vector, P(None, EVERY), vector, vector, vector,
            matrix, vector, matrix, vector,
        ),
        check_vma=False,
    )
```

```python
import functools

import jax
import jax.numpy as jnp
from jax import lax
from jax.experimental import pallas as pl
from jax.experimental.pallas import tpu as pltpu
from jax.sharding import Mesh
from jax.sharding import PartitionSpec as P

HEADS = 16
HD = 128
DOCS = 8
LOG2E = 1.4426950408889634
CHIPS = ("y", "x", "z")
EVERY = ("y", "x", "z", "core")
PAIR = [(0, 1), (1, 0)]
BF16 = jnp.bfloat16
F32 = jnp.float32


def key_place(j, tk, nums, w, i, chips_z, chip_len):
    first = j * tk
    owner = first // chip_len
    slot = lax.rem(nums[w, i, 5] - owner + chips_z, chips_z)
    return slot, pl.multiple_of(first - owner * chip_len, tk), first


def forward_kernel(tq, tk, heads, deps, nums, q_ref, k_ref, v_ref, start_ref, *refs):
    o_ref, lse_ref, acc, top, bias = refs[deps:]
    w, i = pl.program_id(0), pl.program_id(1)
    t0, lo, hi, full_lo, full_hi = (nums[w, i, n] for n in range(5))
    factor = HD**-0.5 * LOG2E
    acc[...] = jnp.zeros_like(acc)
    top[...] = jnp.full_like(top, -1e20)
    ones = jnp.ones((tk, HD), BF16)

    def tile(j, masked):
        slot, row, k0 = key_place(j, tk, nums, w, i, k_ref.shape[0], k_ref.shape[2])
        keys = k_ref[slot, 0, pl.ds(row, tk), :]
        values = jnp.concatenate([v_ref[slot, 0, pl.ds(row, tk), :], ones], axis=1)
        if masked:
            key_pos = k0 + lax.broadcasted_iota(jnp.int32, (tq, tk), 1)
            query_pos = t0 + lax.broadcasted_iota(jnp.int32, (tq, tk), 0)
            allowed = (key_pos <= query_pos) & (key_pos >= start_ref[...][:, :1])
            bias[...] = jnp.where(allowed, 0.0, -1e30)
        for h in range(heads):
            queries = q_ref[:, h * HD : (h + 1) * HD]
            scores = contract_cols(queries, keys) * factor
            if masked:
                scores = scores + bias[...]
            old = top[h]
            new = jnp.maximum(old, jnp.max(scores, axis=1, keepdims=True))
            probs = jnp.exp2(scores - jnp.concatenate([new] * (tk // HD), axis=1)).astype(BF16)
            fade = jnp.exp2(old - new)
            top[h] = new
            acc[h] = acc[h] * jnp.concatenate([fade, fade], axis=1) + plain_dot(probs, values)

    def step(j, carry):
        partial = (j < full_lo) | (j >= full_hi)

        @pl.when(partial)
        def _():
            tile(j, True)

        @pl.when(jnp.logical_not(partial))
        def _():
            tile(j, False)

        return carry

    lax.fori_loop(lo, hi, step, 0)
    lane = lax.broadcasted_iota(jnp.int32, (tq, HD), 1)
    stats = jnp.zeros((tq, HD), F32)
    for h in range(heads):
        total = acc[h, :, HD:]
        o_ref[:, h * HD : (h + 1) * HD] = (acc[h, :, :HD] / total).astype(BF16)
        stats = jnp.where(lane == h, top[h] + jnp.log2(total), stats)
    lse_ref[...] = jnp.transpose(stats)[:heads]


def attend_forward(queries, keys, values, starts, nums, tq, tk, deps=()):
    chips_z, windows, chip_len, _ = keys.shape
    rows, width = queries.shape
    heads = width // HD
    tiles = rows // windows // tq

    def block(w, i):
        return w * tiles + i

    spread = jnp.broadcast_to(starts.reshape(rows, 1), (rows, HD))
    key_spec = pl.BlockSpec((chips_z, 1, chip_len, HD), lambda w, i, n: (0, w, 0, 0))
    return pl.pallas_call(
        functools.partial(forward_kernel, tq, tk, heads, len(deps)),
        grid_spec=pltpu.PrefetchScalarGridSpec(
            num_scalar_prefetch=1,
            grid=(windows, tiles),
            in_specs=[
                pl.BlockSpec((tq, width), lambda w, i, n: (block(w, i), 0)),
                key_spec,
                key_spec,
                pl.BlockSpec((tq, HD), lambda w, i, n: (block(w, i), 0)),
            ]
            + [pl.BlockSpec(memory_space=pl.ANY)] * len(deps),
            out_specs=[
                pl.BlockSpec((tq, width), lambda w, i, n: (block(w, i), 0)),
                pl.BlockSpec((heads, tq), lambda w, i, n: (0, block(w, i))),
            ],
            scratch_shapes=[
                pltpu.VMEM((heads, tq, 2 * HD), F32),
                pltpu.VMEM((heads, tq, HD), F32),
                pltpu.VMEM((tq, tk), F32),
            ],
        ),
        out_shape=[
            jax.ShapeDtypeStruct((rows, width), BF16),
            jax.ShapeDtypeStruct((heads, rows), F32),
        ],
        compiler_params=pltpu.CompilerParams(vmem_limit_bytes=40 * 2**20),
        cost_estimate=pl.CostEstimate(
            flops=2 * rows * width * chip_len * chips_z, bytes_accessed=4 * rows * width,
            transcendentals=rows * heads * chip_len * chips_z // 4,
        ),
        name="attention_forward",
    )(nums, queries, keys, values, spread, *deps)


def backward_kernel(tq, tk, heads, deps, nums, q_ref, g_ref, o_ref, lse_ref, k_ref, v_ref, start_ref, *refs):
    (dq_ref, dk_ref, dv_ref, dq_acc, dk_acc, dv_acc, bias, delta, probs_all, grads_all, q_all, g_all, turned) = refs[deps:]
    w, i = pl.program_id(0), pl.program_id(1)
    t0, lo, hi, full_lo, full_hi = (nums[w, i, n] for n in range(5))
    scale = HD**-0.5
    factor = scale * LOG2E
    chips_z, chip_len = k_ref.shape[0], k_ref.shape[2]

    @pl.when(i == 0)
    def _():
        dk_acc[...] = jnp.zeros_like(dk_acc)
        dv_acc[...] = jnp.zeros_like(dv_acc)
        for s in range(chips_z):
            turned[s] = jnp.transpose(k_ref[s, 0])

    dq_acc[...] = jnp.zeros_like(dq_acc)
    ones = jnp.ones((8, HD), F32)
    for h in range(heads):
        cols = slice(h * HD, (h + 1) * HD)
        rows = slice(h * tq, (h + 1) * tq)
        product = g_ref[:, cols].astype(F32) * o_ref[:, cols].astype(F32)
        delta[h] = lax.dot_general(
            ones, product, (((1,), (1,)), ((), ())), precision=lax.Precision.HIGHEST, preferred_element_type=F32
        )
        q_all[rows, :] = q_ref[:, cols]
        g_all[rows, :] = g_ref[:, cols]

    def tile(j, masked):
        slot, row, k0 = key_place(j, tk, nums, w, i, chips_z, chip_len)
        keys = k_ref[slot, 0, pl.ds(row, tk), :]
        values = v_ref[slot, 0, pl.ds(row, tk), :]
        if masked:
            key_pos = k0 + lax.broadcasted_iota(jnp.int32, (tk, tq), 0)
            query_pos = t0 + lax.broadcasted_iota(jnp.int32, (tk, tq), 1)
            allowed = (key_pos <= query_pos) & (key_pos >= start_ref[:1, :])
            bias[...] = jnp.where(allowed, 0.0, -1e30)
        for h in range(heads):
            rows = slice(h * tq, (h + 1) * tq)
            scores = contract_cols(keys, q_all[rows, :]) * factor
            if masked:
                scores = scores + bias[...]
            probs = jnp.exp2(scores - lse_ref[h : h + 1, :])
            grad_probs = contract_cols(values, g_all[rows, :])
            probs_all[:, rows] = probs.astype(BF16)
            grads_all[:, rows] = (probs * (grad_probs - delta[h, :1, :])).astype(BF16)
        dk_acc[slot, pl.ds(row, tk), :] += plain_dot(grads_all[...], q_all[...])
        dv_acc[slot, pl.ds(row, tk), :] += plain_dot(probs_all[...], g_all[...])
        dq_acc[...] += plain_dot(turned[slot, :, pl.ds(row, tk)], grads_all[...])

    def step(j, carry):
        partial = (j < full_lo) | (j >= full_hi)

        @pl.when(partial)
        def _():
            tile(j, True)

        @pl.when(jnp.logical_not(partial))
        def _():
            tile(j, False)

        return carry

    lax.fori_loop(lo, hi, step, 0)
    for h in range(heads):
        rows = slice(h * tq, (h + 1) * tq)
        dq_ref[:, h * HD : (h + 1) * HD] = (jnp.transpose(dq_acc[:, rows]) * scale).astype(BF16)

    @pl.when(i == pl.num_programs(1) - 1)
    def _():
        dk_ref[:, 0] = (dk_acc[...] * scale).astype(BF16)
        dv_ref[:, 0] = dv_acc[...].astype(BF16)


def attend_backward(queries, grad_attended, first_row, attended, lse, keys, values, starts, nums, tq, tk, deps=()):
    chips_z, windows, chip_len, _ = keys.shape
    rows, width = queries.shape
    heads = width // HD
    tiles = rows // windows // tq
    skip = first_row // tq

    def block(w, i):
        return w * tiles + i

    spread = jnp.broadcast_to(starts.reshape(1, rows), (8, rows))
    row_spec = pl.BlockSpec((tq, width), lambda w, i, n: (block(w, i), 0))
    key_spec = pl.BlockSpec((chips_z, 1, chip_len, HD), lambda w, i, n: (0, w, 0, 0))
    key_shape = jax.ShapeDtypeStruct(keys.shape, BF16)
    return pl.pallas_call(
        functools.partial(backward_kernel, tq, tk, heads, len(deps)),
        grid_spec=pltpu.PrefetchScalarGridSpec(
            num_scalar_prefetch=1,
            grid=(windows, tiles),
            in_specs=[
                row_spec,
                pl.BlockSpec((tq, width), lambda w, i, n: (block(w, i) + skip, 0)),
                row_spec,
                pl.BlockSpec((heads, tq), lambda w, i, n: (0, block(w, i))),
                key_spec,
                key_spec,
                pl.BlockSpec((8, tq), lambda w, i, n: (0, block(w, i))),
            ]
            + [pl.BlockSpec(memory_space=pl.ANY)] * len(deps),
            out_specs=[row_spec, key_spec, key_spec],
            scratch_shapes=[
                pltpu.VMEM((HD, heads * tq), F32),
                pltpu.VMEM((chips_z, chip_len, HD), F32),
                pltpu.VMEM((chips_z, chip_len, HD), F32),
                pltpu.VMEM((tk, tq), F32),
                pltpu.VMEM((heads, 8, tq), F32),
                pltpu.VMEM((tk, heads * tq), BF16),
                pltpu.VMEM((tk, heads * tq), BF16),
                pltpu.VMEM((heads * tq, HD), BF16),
                pltpu.VMEM((heads * tq, HD), BF16),
                pltpu.VMEM((chips_z, HD, chip_len), BF16),
            ],
        ),
        out_shape=[jax.ShapeDtypeStruct((rows, width), BF16), key_shape, key_shape],
        compiler_params=pltpu.CompilerParams(vmem_limit_bytes=40 * 2**20),
        cost_estimate=pl.CostEstimate(
            flops=4 * rows * width * chip_len * chips_z, bytes_accessed=8 * rows * width,
            transcendentals=rows * heads * chip_len * chips_z // 4,
        ),
        name="attention_backward",
    )(nums, queries, grad_attended, attended, lse, keys, values, spread, *deps)


def tile_numbers(starts, positions, z, tq, tk):
    windows, local = starts.shape
    tiled = starts.reshape(windows, local // tq, tq)
    t0 = jnp.broadcast_to(positions.reshape(local // tq, tq)[None, :, 0], (windows, local // tq))
    first, last = tiled[:, :, 0], tiled[:, :, -1]
    return jnp.stack(
        [t0, first // tk, (t0 + tq - 1) // tk + 1, (last + tk - 1) // tk, (t0 + 1) // tk, jnp.broadcast_to(z, t0.shape)],
        axis=2,
    ).astype(jnp.int32)


def store(part, total, extras, outs):
    outs[0][part, :] = total.astype(outs[0].dtype)


def sum_finish(part, total, extras, outs):
    total = total + extras[0][part, :] + extras[1][...] + extras[2][part, :].astype(F32) + extras[3][part, :]
    outs[0][part, :] = total.astype(BF16)


def add_finish(part, total, extras, outs):
    outs[0][part, :] = (total + extras[0][part, :]).astype(outs[0].dtype)


def slope_finish(part, total, extras, outs):
    grad = (total * extras[0][part, :].astype(F32)).astype(BF16)
    outs[0][part, :] = grad
    sums = jnp.sum(grad.astype(F32).reshape(-1, 8, grad.shape[1]), axis=0)
    if part.start == 0:
        outs[1][...] = sums
    else:
        outs[1][...] += sums


def gelu_finish(part, total, extras, outs):
    u = total + extras[0][...]
    square = u * u
    s = 0.5 * jnp.tanh(u * (0.7978845608028654 + (0.7978845608028654 * 0.044715) * square)) + 0.5
    value = u * s
    outs[0][part, :] = value.astype(BF16)
    rate = 2 * 0.7978845608028654 + (6 * 0.7978845608028654 * 0.044715) * square
    outs[1][part, :] = (s + value * (1.0 - s) * rate).astype(BF16)


def rows_kernel(kind, chunk, extra_count, dep_count, finish, a_ref, b_ref, *refs):
    extras, outs = refs[:extra_count], refs[extra_count + dep_count :]
    dot = contract_cols if kind == "nt" else plain_dot
    for r in range(0, a_ref.shape[0], chunk):
        part = pl.ds(r, chunk)
        finish(part, dot(a_ref[part, :], b_ref[...]), extras, outs)


def matmul(
    kind, a, b, outs, finish=store, extras=(), tn=512, chunk=256, deps=(), depth=None, a_part=0, b_part=0, extra_part=0, name="matmul"
):
    m, k = a.shape[0], depth or a.shape[1]
    n = b.shape[0] if kind == "nt" else b.shape[1]
    tn, chunk = min(tn, n), min(chunk, m)
    skip = extra_part * (n // tn)
    given = {"tile": pl.BlockSpec((m, tn), lambda j: (0, j + skip)), "row": pl.BlockSpec((1, tn), lambda j: (0, j + skip))}
    spec = {"tile": pl.BlockSpec((m, tn), lambda j: (0, j)), "sums": pl.BlockSpec((8, tn), lambda j: (0, j))}
    shape = {"tile": (m, n), "sums": (8, n)}
    res = pl.pallas_call(
        functools.partial(rows_kernel, kind, chunk, len(extras), len(deps), finish),
        grid=(n // tn,),
        in_specs=[
            pl.BlockSpec((m, k), lambda j: (0, a_part)),
            pl.BlockSpec((tn, k), lambda j: (j, b_part)) if kind == "nt" else pl.BlockSpec((k, tn), lambda j: (0, j)),
        ]
        + [given[kind_of] for _, kind_of in extras]
        + [pl.BlockSpec(memory_space=pl.ANY)] * len(deps),
        out_specs=[spec[w] for _, w in outs],
        out_shape=[jax.ShapeDtypeStruct(shape[w], d) for d, w in outs],
        compiler_params=pltpu.CompilerParams(vmem_limit_bytes=52 * 2**20),
        cost_estimate=pl.CostEstimate(flops=2 * m * n * k, bytes_accessed=2 * (m * k + n * k + m * n), transcendentals=0),
        name=name,
    )(a, b, *[array for array, _ in extras], *deps)
    return res[0] if len(outs) == 1 else res


def tokens_kernel(chunk, dep_count, a0_ref, a1_ref, b0_ref, b1_ref, *refs):
    out, left = refs[dep_count:]

    @pl.when(pl.program_id(1) == 0)
    def _():
        left[0] = jnp.transpose(a0_ref[...])
        left[1] = jnp.transpose(a1_ref[...])

    for r in range(0, left.shape[1], chunk):
        part = pl.ds(r, chunk)
        out[part, :] = (plain_dot(left[0, part, :], b0_ref[...]) + plain_dot(left[1, part, :], b1_ref[...])).astype(BF16)


def over_tokens(a, b, tm=2048, tn=512, chunk=256, deps=(), a_cols=None, name="weight_gradient"):
    k = a[0].shape[0]
    first, m = a_cols or (0, a[0].shape[1])
    n = b[0].shape[1]
    tm, tn, chunk = min(tm, m), min(tn, n), min(chunk, m)
    skip = first // tm
    a_spec = pl.BlockSpec((k, tm), lambda i, j: (0, i + skip))
    b_spec = pl.BlockSpec((k, tn), lambda i, j: (0, j))
    return pl.pallas_call(
        functools.partial(tokens_kernel, chunk, len(deps)),
        grid=(m // tm, n // tn),
        in_specs=[a_spec, a_spec, b_spec, b_spec] + [pl.BlockSpec(memory_space=pl.ANY)] * len(deps),
        out_specs=pl.BlockSpec((tm, tn), lambda i, j: (i, j)),
        scratch_shapes=[pltpu.VMEM((2, tm, k), BF16)],
        out_shape=jax.ShapeDtypeStruct((m, n), BF16),
        compiler_params=pltpu.CompilerParams(vmem_limit_bytes=52 * 2**20),
        cost_estimate=pl.CostEstimate(flops=4 * m * n * k, bytes_accessed=4 * (m * k + n * k + m * n), transcendentals=0),
        name=name,
    )(*a, *b, *deps)


def contract_rows(left_op, right_op):
    return lax.dot_general(left_op, right_op, (((0,), (0,)), ((), ())), preferred_element_type=F32)


def contract_cols(left_op, right_op):
    return lax.dot_general(left_op, right_op, (((1,), (1,)), ((), ())), preferred_element_type=F32)


def plain_dot(left_op, right_op):
    return jnp.dot(left_op, right_op, preferred_element_type=F32)


def normalise(values):
    centred = values - jnp.mean(values, axis=-1, keepdims=True)
    spread = jnp.mean(centred * centred, axis=-1, keepdims=True)
    inverse = lax.rsqrt(spread + 1e-05)
    return centred * inverse, inverse


def norm_kernel(rounded, dep_count, own_ref, got_ref, unit_ref, inverse_ref, gain_ref, base_ref, *refs):
    outs = refs[dep_count:]
    grad = own_ref[...] + got_ref[...].astype(F32)
    unit = unit_ref[...]
    scaled = grad * gain_ref[...]
    inner = jnp.mean(scaled * unit, axis=-1, keepdims=True)
    level = jnp.mean(scaled, axis=-1, keepdims=True)
    result = base_ref[...].astype(F32) + (scaled - level - unit * inner) * inverse_ref[...][:, :1]
    outs[0][...] = result
    terms = [grad * unit, grad]
    if rounded:
        low = result.astype(BF16)
        outs[3][...] = low
        terms.append(low.astype(F32))
    first = pl.program_id(0) == 0
    for term, out in zip(terms, (outs[1], outs[2], outs[-1])):
        sums = jnp.sum(term.reshape(-1, 8, term.shape[1]), axis=0)

        @pl.when(first)
        def _(out=out, sums=sums):
            out[...] = sums

        @pl.when(jnp.logical_not(first))
        def _(out=out, sums=sums):
            out[...] += sums


def norm_backward(own, got, unit, inverse, gain, base, rounded, deps=()):
    rows, cols = own.shape
    tile = min(128, rows)
    block = pl.BlockSpec((tile, cols), lambda i: (i, 0))
    sums = pl.BlockSpec((8, cols), lambda i: (0, 0))
    sums_shape = jax.ShapeDtypeStruct((8, cols), F32)
    out_specs, out_shape = [block, sums, sums], [jax.ShapeDtypeStruct((rows, cols), F32), sums_shape, sums_shape]
    if rounded:
        out_specs += [block, sums]
        out_shape += [jax.ShapeDtypeStruct((rows, cols), BF16), sums_shape]
    return pl.pallas_call(
        functools.partial(norm_kernel, rounded, len(deps)),
        grid=(rows // tile,),
        in_specs=[
            block, block, block, pl.BlockSpec((tile, HD), lambda i: (i, 0)), pl.BlockSpec((1, cols), lambda i: (0, 0)), block,
        ]
        + [pl.BlockSpec(memory_space=pl.ANY)] * len(deps),
        out_specs=out_specs,
        out_shape=out_shape,
        compiler_params=pltpu.CompilerParams(vmem_limit_bytes=40 * 2**20),
        name="norm_backward",
    )(own, got, unit, jnp.broadcast_to(inverse, (rows, HD)), gain.reshape(1, cols), base, *deps)


def swap(values, axis):
    return lax.ppermute(values, axis, PAIR)


def in_order(index, own, other):
    return jnp.where(index == 0, jnp.stack([own, other]), jnp.stack([other, own]))


def pick(values, index, axis):
    return lax.dynamic_index_in_dim(values, index, axis, keepdims=False)


def exchange_add(values, index, axis_name, dim):
    arrived = swap(pick(values, 1 - index, dim), axis_name)
    return pick(values, index, dim).astype(F32) + arrived.astype(F32)


def core_rows(core, first, second):
    own = jnp.where(core == 0, first, second)
    other = swap(jnp.where(core == 0, second, first), "core")
    return in_order(core, own, other).reshape(2 * own.shape[0], own.shape[1])


def hold_kernel(dep_count, value_ref, *refs):
    refs[dep_count][...] = value_ref[...]


def hold(value, *deps):
    whole = pl.BlockSpec(value.shape, lambda: (0,) * value.ndim)
    return pl.pallas_call(
        functools.partial(hold_kernel, len(deps)),
        in_specs=[whole] + [pl.BlockSpec(memory_space=pl.ANY)] * len(deps),
        out_specs=whole,
        out_shape=jax.ShapeDtypeStruct(value.shape, value.dtype),
        name="hold",
    )(value, *deps)


def place_kernel(moves_of, whole_count, half, dep_count, spot, *refs):
    count = len(moves_of)
    pieces = refs[:count]
    whole = refs[count : count + whole_count]
    out, held, arrive, leave = refs[count + whole_count + dep_count :]
    y, x, z = spot[0], spot[1], spot[2]
    steps = count // 4
    parts = 2 + whole_count * 2
    moves = []
    for n, move in enumerate(moves_of):
        s, k = move
        from_z = lax.rem(z - s + steps, steps)
        for i in range(2):
            to = ((i, x, 0), (i, 1 - x, 0), (y, i, 1), (1 - y, i, 1))[k]
            row = (((to[0] * 2 + to[1]) * steps + from_z) * parts + whole_count * 2 + to[2]) * half
            moves.append((pieces[n].at[i], pl.multiple_of(row, half), half))
    for array in whole:
        for chip in range(4 * steps):
            moves.append((array.at[pl.ds(chip * 2 * half, 2 * half), :], chip * parts * half, 2 * half))
    inward, outward, at = [], [], 0
    for n, (source, row, rows) in enumerate(moves):
        here = held.at[pl.ds(at, rows), :]
        inward.append(pltpu.make_async_copy(source, here, arrive.at[n]))
        outward.append(pltpu.make_async_copy(here, out.at[pl.ds(row, rows), :], leave.at[n]))
        at += rows
    for copy in inward:
        copy.start()
    for n, copy in enumerate(inward):
        copy.wait()
        outward[n].start()
    for copy in outward:
        copy.wait()


def place(pieces, spot, whole=(), deps=()):
    steps = len(pieces) // 4
    _, half, cols = pieces[0].shape
    count = 8 * steps + 4 * steps * len(whole)
    rows = 8 * steps * half * (1 + len(whole))
    moves_of = [(s, k) for s in range(steps) for k in range(4)]
    return pl.pallas_call(
        functools.partial(place_kernel, moves_of, len(whole), half, len(deps)),
        grid_spec=pltpu.PrefetchScalarGridSpec(
            num_scalar_prefetch=1,
            grid=(1,),
            in_specs=[pl.BlockSpec(memory_space=pl.ANY)] * (len(pieces) + len(whole) + len(deps)),
            out_specs=pl.BlockSpec(memory_space=pl.ANY),
            scratch_shapes=[
                pltpu.VMEM((rows, cols), BF16),
                pltpu.SemaphoreType.DMA((count,)),
                pltpu.SemaphoreType.DMA((count,)),
            ],
        ),
        out_shape=jax.ShapeDtypeStruct((rows, cols), BF16),
        compiler_params=pltpu.CompilerParams(vmem_limit_bytes=32 * 2**20),
        name="place_weight",
    )(spot, *pieces, *whole, *deps)


def gather_pieces(block, y, x, chips_z):
    half = block.shape[0] // 2
    ring = [(i, (i + 1) % chips_z) for i in range(chips_z)]
    one, two = block[:half], block[half:]
    got_one, got_two = swap(one, "y"), swap(two, "x")
    one, two = in_order(y, one, got_one), in_order(x, two, got_two)
    pieces, stages = [], []
    for s in range(chips_z):
        stages.append((one, two))
        pieces += [one, swap(one, "x"), two, swap(two, "y")]
        if s < chips_z - 1:
            one, two = lax.ppermute(one, "z", ring), lax.ppermute(two, "z", ring)
    return pieces, stages


def fold_kernel(spot, own_one, own_two, got_one, got_two, *refs):
    keep_one, send_one, keep_two, send_two = refs[-4:]
    y, x = spot[0], spot[1]
    for mine, own, got, keep, send in ((x, own_one, got_one, keep_one, send_one), (y, own_two, got_two, keep_two, send_two)):
        for index, out in ((mine, keep), (1 - mine, send)):
            total = own[own_at(own, index)].astype(F32) + got[index, 0].astype(F32)
            out[0] = total.astype(BF16)


def own_at(ref, index):
    return (index, 0, 0, 0) if ref.shape[0] == 2 else (0, index, 0, 0)


def fold_again_kernel(count, *refs):
    out = refs[-1]
    cols = out.shape[-1] // count
    for n in range(count):
        keep_one, keep_two, got_one, got_two = refs[4 * n : 4 * n + 4]
        here = pl.ds(n * cols, cols)
        out[0, 0, :, here] = (keep_one[0].astype(F32) + got_one[0].astype(F32)).astype(BF16)
        out[0, 1, :, here] = (keep_two[0].astype(F32) + got_two[0].astype(F32)).astype(BF16)


class Sum:
    def __init__(self, total, spot, chips_z):
        self.cols = total.shape[1]
        self.half = total.shape[0] // (8 * chips_z)
        self.total, self.spot, self.chips_z = total.reshape(2, 2, chips_z, 2, self.half, self.cols), spot, chips_z
        self.sent = (self.cut(0, 1 - spot[0], 0), self.cut(1, 1 - spot[1], 1))

    def cut(self, dim, index, part):
        at, size = [0, 0, 0, part, 0, 0], [2, 2, self.chips_z, 1, self.half, self.cols]
        at[dim], size[dim] = index, 1
        return lax.dynamic_slice(self.total, at, size).reshape(2, self.chips_z, self.half, self.cols)

    def first(self, *deps):
        got = (swap(self.sent[0], "y"), swap(self.sent[1], "x"))
        block = (self.half, self.cols)
        got_spec = pl.BlockSpec((2, 1, *block), lambda z, spot: (0, z, 0, 0))
        out_spec = pl.BlockSpec((1, *block), lambda z, spot: (z, 0, 0))
        keep_one, send_one, keep_two, send_two = pl.pallas_call(
            fold_kernel,
            grid_spec=pltpu.PrefetchScalarGridSpec(
                num_scalar_prefetch=1,
                grid=(self.chips_z,),
                in_specs=[
                    pl.BlockSpec((1, 2, 1, 1, *block), lambda z, spot: (spot[0], 0, z, 0, 0, 0)),
                    pl.BlockSpec((2, 1, 1, 1, *block), lambda z, spot: (0, spot[1], z, 1, 0, 0)),
                    got_spec,
                    got_spec,
                ]
                + [pl.BlockSpec(memory_space=pl.ANY)] * len(deps),
                out_specs=[out_spec] * 4,
            ),
            out_shape=[jax.ShapeDtypeStruct((self.chips_z, *block), BF16)] * 4,
            compiler_params=pltpu.CompilerParams(vmem_limit_bytes=32 * 2**20),
            name="fold",
        )(self.spot, self.total, self.total, *got, *deps)
        self.keep, self.sent = (keep_one, keep_two), (send_one, send_two)

    def second(self, *deps, beside=()):
        sums = (self, *beside)
        arrays = []
        for one in sums:
            arrays += [*one.keep, swap(one.sent[0], "x"), swap(one.sent[1], "y")]
        self.cols *= len(sums)
        self.both = pl.pallas_call(
            functools.partial(fold_again_kernel, len(sums)),
            grid=(self.chips_z,),
            in_specs=[pl.BlockSpec((1, *array.shape[1:]), lambda z: (z, 0, 0)) for array in arrays]
            + [pl.BlockSpec(memory_space=pl.ANY)] * len(deps),
            out_specs=pl.BlockSpec((1, 2, self.half, self.cols), lambda z: (z, 0, 0, 0)),
            out_shape=jax.ShapeDtypeStruct((self.chips_z, 2, self.half, self.cols), BF16),
            compiler_params=pltpu.CompilerParams(vmem_limit_bytes=32 * 2**20),
            name="fold_again",
        )(*arrays, *deps).reshape(-1, self.cols)

    def round_z(self, ring):
        z = self.spot[2]
        both = self.both.reshape(self.chips_z, -1, self.cols)
        running = pick(both, (z + self.chips_z - 1) % self.chips_z, 0)
        for s in range(2, self.chips_z + 1):
            mine = pick(both, (z + self.chips_z - s) % self.chips_z, 0)
            total = mine.astype(F32) + lax.ppermute(running, "z", ring).astype(F32)
            running = total.astype(BF16)
        return total

    def over_z(self):
        self.result = lax.psum_scatter(self.both, "z", scatter_dimension=0, tiled=True)
        return self.result.astype(F32)


def pack_kernel(spot, gain1, bias1, query0, query1, out_bias, gain2, bias2, down_bias, *refs):
    *units, packed = refs
    width = packed.shape[1]
    core = spot[0]
    packed[...] = jnp.zeros_like(packed)
    for n, ref in enumerate((gain1, bias1, out_bias, gain2, bias2, down_bias)):
        packed[n : n + 1, :] = jnp.sum(ref[...], axis=0, keepdims=True)
    count = len(units) // 2
    for n in range(count):
        total = units[2 * n][...] + units[2 * n + 1][...]
        packed[pl.ds(8 + core * count + n, 1), : total.shape[1]] = jnp.sum(total, axis=0, keepdims=True)
    columns = jnp.sum(query0[...], axis=0, keepdims=True) + jnp.sum(query1[...], axis=0, keepdims=True)
    half = width // 2
    for n in range(2):
        packed[6:7, n * half : (n + 1) * half] = jnp.where(core == n, columns[:, :half], 0.0)
    packed[7:8, :HD] = jnp.where(core == 0, 0.0, columns[:, half:])


def pack(core, *arrays):
    width = arrays[0].shape[1]
    units = (len(arrays) - 8) // 2
    return pl.pallas_call(
        pack_kernel,
        grid_spec=pltpu.PrefetchScalarGridSpec(
            num_scalar_prefetch=1,
            grid=(1,),
            in_specs=[pl.BlockSpec(a.shape, lambda i, spot: (0, 0)) for a in arrays],
            out_specs=pl.BlockSpec((8 + 2 * units, width), lambda i, spot: (0, 0)),
        ),
        out_shape=jax.ShapeDtypeStruct((8 + 2 * units, width), F32),
        compiler_params=pltpu.CompilerParams(vmem_limit_bytes=32 * 2**20),
        name="pack_small",
    )(core.reshape(1).astype(jnp.int32), *arrays)


def doubling(axis):
    size = lax.axis_size(axis)
    step = 1
    while step < size:
        yield step, [(i, i ^ step) for i in range(size)]
        step *= 2


def gather_small(vector):
    for axis in reversed(EVERY):
        index = lax.axis_index(axis)
        for step, pairs in doubling(axis):
            vector = in_order((index // step) % 2, vector, lax.ppermute(vector, axis, pairs))
    return vector.reshape(-1, vector.shape[-1])


def sum_small(vector):
    for axis in reversed(EVERY):
        for _, pairs in doubling(axis):
            vector = vector + lax.ppermute(vector, axis, pairs)
    return vector


def join_kernel(cut, core, own, other, out):
    cols = own.shape[1]
    rest = cols - cut
    for n in range(2):
        for index, ref in ((n, own), (1 - n, other)):

            @pl.when(core[0] == n)
            def _(index=index, ref=ref):
                out[:, index * cut : (index + 1) * cut] = ref[:, :cut]
                out[:, 2 * cut + index * rest : 2 * cut + (index + 1) * rest] = ref[:, cut:]


def join_columns(core, own, other, cut):
    rows, cols = own.shape
    whole = pl.BlockSpec((rows, cols), lambda i, spot: (0, 0))
    return pl.pallas_call(
        functools.partial(join_kernel, cut),
        grid_spec=pltpu.PrefetchScalarGridSpec(
            num_scalar_prefetch=1,
            grid=(1,),
            in_specs=[whole, whole],
            out_specs=pl.BlockSpec((rows, 2 * cols), lambda i, spot: (0, 0)),
        ),
        out_shape=jax.ShapeDtypeStruct((rows, 2 * cols), F32),
        name="join_columns",
    )(core.reshape(1).astype(jnp.int32), own, other)


def own_rows(core, rows):
    pair = rows.reshape(2, rows.shape[0] // 2, rows.shape[1])
    own = pick(pair, core, 0)
    other = swap(pick(pair, 1 - core, 0), "core")
    return in_order(core, own, other)


def body(
    hidden_in, doc_lengths, cotangent, ln1_gain, ln1_bias, w_qkv, b_qv, w_out, b_out,
    ln2_gain, ln2_bias, w_up, b_up, w_down, b_down,
):
    windows, local_len, width = hidden_in.shape
    own_count = windows * local_len
    count = 2 * own_count
    chips_z = lax.axis_size("z")
    chips = 2 * lax.axis_size("y") * chips_z
    y, x, z, core = (lax.axis_index(name) for name in EVERY)
    width_q = HEADS * HD
    half_q = width_q // 2
    chip_len = 2 * local_len
    length = chip_len * chips_z
    hidden_units = w_up.shape[1]
    unit_block = hidden_units // (2 * chips)

    doc_ends = jnp.cumsum(doc_lengths, axis=1)
    cores = jnp.stack([core, 1 - core])
    positions = (z * chip_len + cores[:, None] * local_len + jnp.arange(local_len, dtype=jnp.int32)[None, :]).astype(jnp.int32)
    ended = positions[:, None, :, None] >= doc_ends[None, :, None, :]
    starts = jnp.max(jnp.where(ended, doc_ends[None, :, None, :], 0), axis=3)
    valid = (jnp.sum(ended[0].astype(jnp.int32), axis=2) < DOCS).reshape(own_count, 1)

    vectors = (ln1_gain, ln1_bias, b_qv, b_out, ln2_gain, ln2_bias, b_up, b_down)
    sizes = [v.shape[0] for v in vectors]
    packed = gather_small(jnp.concatenate(vectors)).astype(F32)
    full = []
    at = 0
    for size in sizes:
        full.append(packed[:, at : at + size].reshape(-1))
        at += size
    gain1, bias1, bias_qv, bias_out, gain2, bias2, bias_up, bias_down = full
    bias_up = jnp.swapaxes(pick(bias_up.reshape(chips, 2, 2, unit_block // 2), core, 1), 0, 1).reshape(-1)
    bias_qkv = jnp.where(
        core == 0,
        jnp.concatenate([bias_qv[:half_q], jnp.zeros((HD,), F32)]),
        jnp.concatenate([bias_qv[half_q:width_q], bias_qv[width_q:]]),
    )
    w_out_t = w_out.T
    near_block = core_rows(
        core,
        jnp.concatenate([w_qkv[:, :half_q], w_qkv[:, width_q : width_q + HD], w_out_t[:, :half_q]], axis=1),
        jnp.concatenate([w_qkv[:, half_q:width_q], w_qkv[:, width_q + HD :], w_out_t[:, half_q:]], axis=1),
    )
    up_parts = jnp.moveaxis(w_up.reshape(w_up.shape[0], chips, 2, 2, unit_block // 2), 3, 1)
    up_block = core_rows(
        core,
        up_parts[:, :, :, 0].reshape(w_up.shape[0], -1),
        up_parts[:, :, :, 1].reshape(w_up.shape[0], -1),
    )
    spot = jnp.stack([y, x, z]).astype(jnp.int32)
    by_hand = lax.axis_size("y") == 2
    ring = [(i, (i + 1) % chips_z) for i in range(chips_z)]

    def gather(block):
        return lax.all_gather(block, CHIPS, axis=0, tiled=True)

    def both_cores(own):
        return (own, swap(own, "core"))

    near_all, w_up_all = gather(near_block), gather(up_block)
    w_out_all = near_all[:, half_q + HD :]

    tokens = hidden_in.reshape(own_count, width).astype(F32)
    unit1, inverse1 = normalise(tokens)
    normed1 = both_cores((unit1 * gain1 + bias1).astype(BF16))
    w_query, w_kv = near_all[:, :half_q], near_all[:, half_q : half_q + HD]
    own_kv = [(plain_dot(rows, w_kv) + bias_qkv[half_q:]).astype(BF16) for rows in normed1]
    own_kv = [rows.reshape(windows, local_len, HD) for rows in own_kv]
    own_kv = jnp.swapaxes(in_order(core, *own_kv), 0, 1).reshape(windows, chip_len, HD)
    keys, values = [], []
    for s in range(chips_z):
        other_kv = swap(own_kv, "core")
        keys.append(jnp.where(core == 0, own_kv, other_kv))
        values.append(jnp.where(core == 0, other_kv, own_kv))
        if s < chips_z - 1:
            own_kv = lax.ppermute(own_kv, "z", ring)
    down_rows = w_down.shape[0] // 2
    w_down_parts = [gather(w_down[:down_rows]), gather(w_down[down_rows:])]
    keys, values = jnp.stack(keys), jnp.stack(values)
    queries = [(plain_dot(rows, w_query) + bias_qkv[:half_q]).astype(BF16) for rows in normed1]
    tq_forward, tk_forward = min(512, local_len), min(512, chip_len)
    tq, tk = min(256, local_len), min(256, chip_len)
    attended, lse = [None, None], [None, None]
    for n in (1, 0):
        attended[n], lse[n] = attend_forward(
            queries[n], keys, values, starts[n],
            tile_numbers(starts[n], positions[n], z, tq_forward, tk_forward), tq_forward, tk_forward,
            () if n == 1 else (attended[1],),
        )
        if n == 1:
            out_other = swap(matmul("nt", attended[1], w_out_all, [(BF16, "tile")], name="attention_out"), "core")
    residual = tokens + bias_out + contract_cols(attended[0], w_out_all) + out_other.astype(F32)

    unit2, inverse2 = normalise(residual)
    normed2 = both_cores((unit2 * gain2 + bias2).astype(BF16))
    active, slope = [None, None], [None, None]
    for n in (0, 1):
        active[n], slope[n] = matmul(
            "nn", normed2[n], w_up_all, [(BF16, "tile"), (BF16, "tile")], gelu_finish, [(bias_up.reshape(1, -1), "row")],
            name="upward",
        )
    upstream = jnp.where(valid, cotangent.reshape(own_count, width), 0)
    grad_down = both_cores(upstream)
    units = active[0].shape[1] // 2
    down_totals = [over_tokens(active, grad_down, a_cols=(n * units, units), name="grad_w_down") for n in (0, 1)]
    down_sums = [Sum(total, spot, chips_z) for total in down_totals] if by_hand else ()

    grad_up, unit_sums, up_totals, up_sums = [None, None], [], [], []
    grad_normed, down_out = [None, None], [None, None]
    deps = tuple(array for one in down_sums for array in one.sent)
    for part in (0, 1):
        for n in (0, 1):
            grad_up[n], sums = matmul(
                "nt", grad_down[n], w_down_parts[part], [(BF16, "tile"), (F32, "sums")], slope_finish, [(slope[n], "tile")],
                extra_part=part, deps=deps, name="grad_up",
            )
            unit_sums.append(sums)
        up_totals.append(over_tokens(normed2, grad_up, name="grad_w_up"))
        deps = (up_totals[-1],)
        if by_hand:
            up_sums.append(Sum(up_totals[-1], spot, chips_z))
            deps += up_sums[-1].sent
            if part == 1:
                down_sums[0].second(up_totals[1], beside=down_sums[1:])
                grad_w_down = down_sums[0].over_z()
                up_sums[0].first(up_totals[1])
                deps += (down_sums[0].both,) + up_sums[0].sent
        for n in (1, 0):
            grad_normed[n] = matmul(
                "nt", grad_up[n], w_up_all, [(F32 if n == 0 or part == 0 else BF16, "tile")],
                add_finish if part else store, [(grad_normed[n], "tile")] if part else (), depth=units, b_part=part,
                deps=deps, name="grad_normed2",
            )
            deps = (grad_normed[n],)
        for n in (1, 0)[: 2 - part]:
            down_out[n] = matmul(
                "nn", active[n], w_down_parts[part], [(BF16 if part else F32, "tile")], add_finish if part else store,
                [(down_out[n], "tile")] if part else (), depth=units, a_part=part, deps=deps, name="mixed_out",
            )
            deps = (down_out[n],)
        if by_hand and part == 0:
            for one in down_sums:
                one.first(down_out[0])
            deps += tuple(array for one in down_sums for array in one.sent)
    mixed_other, mixed_own = grad_normed[1], grad_normed[0]
    down_other = down_out[1]
    grad_residual, gain2_sums, bias2_sums, branch_own, out_sums = norm_backward(
        mixed_own, swap(mixed_other, "core"), unit2, inverse2, gain2, upstream, True, deps
    )
    branch = both_cores(branch_own)

    grad_attended = [matmul("nn", branch[n], w_out_all, [(BF16, "tile")], name="grad_attended") for n in (0, 1)]
    out_total = over_tokens(branch, attended, deps=(grad_attended[1],), name="grad_w_out")
    if by_hand:
        out_sum = Sum(out_total, spot, chips_z)
        up_sums[1].first(out_total)
    grad_query, grad_keys, grad_values = [None, None], [None, None], [None, None]
    for n in (0, 1):
        deps = ()
        if by_hand:
            if n == 0:
                deps = out_sum.sent + up_sums[1].sent
            else:
                up_sums[0].second(grad_keys[0], beside=up_sums[1:])
                grad_w_up = up_sums[0].over_z()
                deps = (up_sums[0].both, down_sums[0].result)
        grad_query[n], grad_keys[n], grad_values[n] = attend_backward(
            queries[n], grad_attended[n], 0, attended[n], lse[n], keys, values, starts[n],
            tile_numbers(starts[n], positions[n], z, tq, tk), tq, tk, deps,
        )
    if by_hand:
        out_sum.first(grad_keys[1])
    grad_keys = grad_keys[0].astype(F32) + grad_keys[1].astype(F32)
    grad_values = grad_values[0].astype(F32) + grad_values[1].astype(F32)
    kv_sent = jnp.where(core == 0, grad_values, grad_keys).astype(BF16)
    query_total = over_tokens(
        normed1, grad_query, deps=(kv_sent,), name="grad_w_query"
    )
    grad_kv = (jnp.where(core == 0, grad_keys, grad_values) + swap(kv_sent, "core").astype(F32)).astype(BF16)
    running = hold(grad_kv[1 % chips_z], query_total, *((up_sums[0].result,) if by_hand else ()))
    for s in range(2, chips_z + 1):
        running = (grad_kv[s % chips_z].astype(F32) + lax.ppermute(running, "z", ring).astype(F32)).astype(BF16)
    grad_kv = jnp.swapaxes(running.reshape(windows, 2, local_len, HD), 0, 1)
    grad_kv = in_order(core, grad_kv[0], grad_kv[1]).reshape(2, own_count, HD)
    kv_total = (contract_rows(normed1[0], grad_kv[0]) + contract_rows(normed1[1], grad_kv[1])).astype(BF16)
    qkv_total = jnp.concatenate([query_total, kv_total], axis=1)
    mixed_out = matmul(
        "nn", active[0], w_down_parts[1], [(BF16, "tile")], sum_finish,
        [(residual, "tile"), (bias_down.reshape(1, -1), "row"), (swap(down_other, "core"), "tile"), (down_out[0], "tile")],
        depth=units, a_part=1, deps=(query_total,), name="mixed_out",
    )
    grad_qkv = [jnp.concatenate([grad_query[n], grad_kv[n]], axis=1) for n in (0, 1)]
    deps = (mixed_out,)
    if by_hand:
        out_sum.second(mixed_out)
        grad_w_out = out_sum.over_z()
        qkv_sum = Sum(qkv_total, spot, chips_z)
        deps += qkv_sum.sent + (out_sum.both,)
    first_other = matmul("nt", grad_qkv[1], near_all, [(BF16, "tile")], deps=deps, name="grad_normed1")
    first_own = matmul("nt", grad_qkv[0], near_all, [(F32, "tile")], deps=(first_other,), name="grad_normed1")
    grad_hidden, gain1_sums, bias1_sums = norm_backward(
        first_own, swap(first_other, "core"), unit1, inverse1, gain1, grad_residual, False
    )
    if by_hand:
        qkv_sum.first(gain1_sums)
        qkv_sum.second()
        grad_w_qkv = qkv_sum.round_z(ring)
    qkv_sums = [jnp.sum(rows.astype(F32).reshape(-1, 8, rows.shape[1]), axis=0) for rows in grad_qkv]
    upstream_sums = jnp.sum(upstream.astype(F32).reshape(-1, 8, width), axis=0)

    if not by_hand:
        grad_w_down, grad_w_up, grad_w_out, grad_w_qkv = (
            lax.psum_scatter(total, CHIPS, scatter_dimension=0, tiled=True).astype(F32)
            for total in (jnp.concatenate(down_totals, axis=1), jnp.concatenate(up_totals, axis=1), out_total, qkv_total)
        )
    device = ((y * 2 + x) * chips_z + z) * 2 + core
    share = width // (2 * chips)
    sums = sum_small(
        pack(
            core, gain1_sums, bias1_sums, *qkv_sums, out_sums, gain2_sums, bias2_sums, upstream_sums, *unit_sums,
        )
    )
    vectors = lax.dynamic_slice(sums, (0, device * share), (7, share))
    value_bias = lax.dynamic_slice(sums, (7, device * (HD // (2 * chips))), (1, HD // (2 * chips)))[0]
    half_block = unit_block // 2
    unit_bias = lax.dynamic_slice(
        sums, (8 + 2 * core, ((y * 2 + x) * chips_z + z) * half_block), (2, half_block)
    ).reshape(-1)
    grad_w_down = jnp.concatenate([grad_w_down[:, :width], grad_w_down[:, width:]], axis=0)
    pair = grad_w_qkv.reshape(2, -1, half_q + HD)
    own_qkv = join_columns(core, pick(pair, core, 0), swap(pick(pair, 1 - core, 0), "core"), half_q)
    own_out = own_rows(core, grad_w_out)
    own_out = jnp.concatenate([own_out[0], own_out[1]], axis=1).T
    own_up = own_rows(core, grad_w_up)
    own_up = own_up.reshape(2, own_up.shape[1], 2, chips, half_block)
    own_up = jnp.transpose(own_up, (1, 3, 0, 2, 4)).reshape(own_up.shape[1], -1)
    return (
        mixed_out.reshape(windows, local_len, width),
        grad_hidden.reshape(windows, local_len, width),
        vectors[0], vectors[1], own_qkv, vectors[6], value_bias, own_out, vectors[2], vectors[3], vectors[4],
        own_up, unit_bias, grad_w_down, vectors[5],
    )


def solution(mesh):
    split = Mesh(mesh.devices.reshape(mesh.shape["dp"] // 2, 2, mesh.shape["seq"] // 2, 2), EVERY)
    rows = ("y", "x")
    cols = ("z", "core")
    vector, matrix = P(EVERY), P(EVERY, None)
    tokens = P(rows, cols, None)
    return jax.shard_map(
        body,
        mesh=split,
        in_specs=(
            tokens, P(rows, None), tokens, vector, vector, matrix, vector, P(None, EVERY), vector,
            vector, vector, matrix, vector, matrix, vector,
        ),
        out_specs=(
            tokens, tokens, vector, vector, matrix, vector, vector, P(None, EVERY), vector, vector, vector,
            matrix, vector, matrix, vector,
        ),
        check_vma=False,
    )
```

```python
import functools

import jax
import jax.numpy as jnp
from jax import lax
from jax.experimental import pallas as pl
from jax.experimental.pallas import tpu as pltpu
from jax.sharding import Mesh
from jax.sharding import PartitionSpec as P

HEADS = 16
HD = 128
DOCS = 8
LOG2E = 1.4426950408889634
CHIPS = ("y", "x", "z")
EVERY = ("y", "x", "z", "core")
PAIR = [(0, 1), (1, 0)]
BF16 = jnp.bfloat16
F32 = jnp.float32
COST_SCALE = 8


def estimate(flops, bytes_accessed, transcendentals):
    return pl.CostEstimate(
        flops=flops // COST_SCALE, bytes_accessed=bytes_accessed // COST_SCALE, transcendentals=transcendentals // COST_SCALE
    )


def key_place(j, tk, nums, w, i, chips_z, chip_len):
    first = j * tk
    owner = first // chip_len
    slot = lax.rem(nums[w, i, 5] - owner + chips_z, chips_z)
    return slot, pl.multiple_of(first - owner * chip_len, tk), first


def forward_kernel(tq, tk, heads, deps, nums, q_ref, k_ref, v_ref, start_ref, *refs):
    o_ref, lse_ref, acc, top, bias = refs[deps:]
    w, i = pl.program_id(0), pl.program_id(1)
    t0, lo, hi, full_lo, full_hi = (nums[w, i, n] for n in range(5))
    factor = HD**-0.5 * LOG2E
    acc[...] = jnp.zeros_like(acc)
    top[...] = jnp.full_like(top, -1e20)
    ones = jnp.ones((tk, HD), BF16)

    def tile(j, masked):
        slot, row, k0 = key_place(j, tk, nums, w, i, k_ref.shape[0], k_ref.shape[2])
        keys = k_ref[slot, 0, pl.ds(row, tk), :]
        values = jnp.concatenate([v_ref[slot, 0, pl.ds(row, tk), :], ones], axis=1)
        if masked:
            key_pos = k0 + lax.broadcasted_iota(jnp.int32, (tq, tk), 1)
            query_pos = t0 + lax.broadcasted_iota(jnp.int32, (tq, tk), 0)
            allowed = (key_pos <= query_pos) & (key_pos >= start_ref[...][:, :1])
            bias[...] = jnp.where(allowed, 0.0, -1e30)
        for h in range(heads):
            queries = q_ref[:, h * HD : (h + 1) * HD]
            scores = contract_cols(queries, keys) * factor
            if masked:
                scores = scores + bias[...]
            old = top[h]
            new = jnp.maximum(old, jnp.max(scores, axis=1, keepdims=True))
            probs = jnp.exp2(scores - jnp.concatenate([new] * (tk // HD), axis=1)).astype(BF16)
            fade = jnp.exp2(old - new)
            top[h] = new
            acc[h] = acc[h] * jnp.concatenate([fade, fade], axis=1) + plain_dot(probs, values)

    def step(j, carry):
        partial = (j < full_lo) | (j >= full_hi)

        @pl.when(partial)
        def _():
            tile(j, True)

        @pl.when(jnp.logical_not(partial))
        def _():
            tile(j, False)

        return carry

    lax.fori_loop(lo, hi, step, 0)
    lane = lax.broadcasted_iota(jnp.int32, (tq, HD), 1)
    stats = jnp.zeros((tq, HD), F32)
    for h in range(heads):
        total = acc[h, :, HD:]
        o_ref[:, h * HD : (h + 1) * HD] = (acc[h, :, :HD] / total).astype(BF16)
        stats = jnp.where(lane == h, top[h] + jnp.log2(total), stats)
    lse_ref[...] = jnp.transpose(stats)[:heads]


def attend_forward(queries, keys, values, starts, nums, tq, tk, deps=()):
    chips_z, windows, chip_len, _ = keys.shape
    rows, width = queries.shape
    heads = width // HD
    tiles = rows // windows // tq

    def block(w, i):
        return w * tiles + i

    spread = jnp.broadcast_to(starts.reshape(rows, 1), (rows, HD))
    key_spec = pl.BlockSpec((chips_z, 1, chip_len, HD), lambda w, i, n: (0, w, 0, 0))
    return pl.pallas_call(
        functools.partial(forward_kernel, tq, tk, heads, len(deps)),
        grid_spec=pltpu.PrefetchScalarGridSpec(
            num_scalar_prefetch=1,
            grid=(windows, tiles),
            in_specs=[
                pl.BlockSpec((tq, width), lambda w, i, n: (block(w, i), 0)),
                key_spec,
                key_spec,
                pl.BlockSpec((tq, HD), lambda w, i, n: (block(w, i), 0)),
            ]
            + [pl.BlockSpec(memory_space=pl.ANY)] * len(deps),
            out_specs=[
                pl.BlockSpec((tq, width), lambda w, i, n: (block(w, i), 0)),
                pl.BlockSpec((heads, tq), lambda w, i, n: (0, block(w, i))),
            ],
            scratch_shapes=[
                pltpu.VMEM((heads, tq, 2 * HD), F32),
                pltpu.VMEM((heads, tq, HD), F32),
                pltpu.VMEM((tq, tk), F32),
            ],
        ),
        out_shape=[
            jax.ShapeDtypeStruct((rows, width), BF16),
            jax.ShapeDtypeStruct((heads, rows), F32),
        ],
        compiler_params=pltpu.CompilerParams(vmem_limit_bytes=40 * 2**20),
        cost_estimate=estimate(
            flops=2 * rows * width * chip_len * chips_z, bytes_accessed=4 * rows * width,
            transcendentals=rows * heads * chip_len * chips_z // 4,
        ),
        name="attention_forward",
    )(nums, queries, keys, values, spread, *deps)


def backward_kernel(tq, tk, heads, deps, nums, q_ref, g_ref, o_ref, lse_ref, k_ref, v_ref, start_ref, *refs):
    (dq_ref, dk_ref, dv_ref, dq_acc, dk_acc, dv_acc, bias, delta, probs_all, grads_all, q_all, g_all, turned) = refs[deps:]
    w, i = pl.program_id(0), pl.program_id(1)
    t0, lo, hi, full_lo, full_hi = (nums[w, i, n] for n in range(5))
    scale = HD**-0.5
    factor = scale * LOG2E
    chips_z, chip_len = k_ref.shape[0], k_ref.shape[2]

    @pl.when(i == 0)
    def _():
        dk_acc[...] = jnp.zeros_like(dk_acc)
        dv_acc[...] = jnp.zeros_like(dv_acc)
        for s in range(chips_z):
            turned[s] = jnp.transpose(k_ref[s, 0])

    dq_acc[...] = jnp.zeros_like(dq_acc)
    ones = jnp.ones((8, HD), F32)
    for h in range(heads):
        cols = slice(h * HD, (h + 1) * HD)
        rows = slice(h * tq, (h + 1) * tq)
        product = g_ref[:, cols].astype(F32) * o_ref[:, cols].astype(F32)
        delta[h] = lax.dot_general(
            ones, product, (((1,), (1,)), ((), ())), precision=lax.Precision.HIGHEST, preferred_element_type=F32
        )
        q_all[rows, :] = q_ref[:, cols]
        g_all[rows, :] = g_ref[:, cols]

    def tile(j, masked):
        slot, row, k0 = key_place(j, tk, nums, w, i, chips_z, chip_len)
        keys = k_ref[slot, 0, pl.ds(row, tk), :]
        values = v_ref[slot, 0, pl.ds(row, tk), :]
        if masked:
            key_pos = k0 + lax.broadcasted_iota(jnp.int32, (tk, tq), 0)
            query_pos = t0 + lax.broadcasted_iota(jnp.int32, (tk, tq), 1)
            allowed = (key_pos <= query_pos) & (key_pos >= start_ref[:1, :])
            bias[...] = jnp.where(allowed, 0.0, -1e30)
        for h in range(heads):
            rows = slice(h * tq, (h + 1) * tq)
            scores = contract_cols(keys, q_all[rows, :]) * factor
            if masked:
                scores = scores + bias[...]
            probs = jnp.exp2(scores - lse_ref[h : h + 1, :])
            grad_probs = contract_cols(values, g_all[rows, :])
            probs_all[:, rows] = probs.astype(BF16)
            grads_all[:, rows] = (probs * (grad_probs - delta[h, :1, :])).astype(BF16)
        dk_acc[slot, pl.ds(row, tk), :] += plain_dot(grads_all[...], q_all[...])
        dv_acc[slot, pl.ds(row, tk), :] += plain_dot(probs_all[...], g_all[...])
        dq_acc[...] += plain_dot(turned[slot, :, pl.ds(row, tk)], grads_all[...])

    def step(j, carry):
        partial = (j < full_lo) | (j >= full_hi)

        @pl.when(partial)
        def _():
            tile(j, True)

        @pl.when(jnp.logical_not(partial))
        def _():
            tile(j, False)

        return carry

    lax.fori_loop(lo, hi, step, 0)
    for h in range(heads):
        rows = slice(h * tq, (h + 1) * tq)
        dq_ref[:, h * HD : (h + 1) * HD] = (jnp.transpose(dq_acc[:, rows]) * scale).astype(BF16)

    @pl.when(i == pl.num_programs(1) - 1)
    def _():
        dk_ref[:, 0] = (dk_acc[...] * scale).astype(BF16)
        dv_ref[:, 0] = dv_acc[...].astype(BF16)


def attend_backward(queries, grad_attended, first_row, attended, lse, keys, values, starts, nums, tq, tk, deps=()):
    chips_z, windows, chip_len, _ = keys.shape
    rows, width = queries.shape
    heads = width // HD
    tiles = rows // windows // tq
    skip = first_row // tq

    def block(w, i):
        return w * tiles + i

    spread = jnp.broadcast_to(starts.reshape(1, rows), (8, rows))
    row_spec = pl.BlockSpec((tq, width), lambda w, i, n: (block(w, i), 0))
    key_spec = pl.BlockSpec((chips_z, 1, chip_len, HD), lambda w, i, n: (0, w, 0, 0))
    key_shape = jax.ShapeDtypeStruct(keys.shape, BF16)
    return pl.pallas_call(
        functools.partial(backward_kernel, tq, tk, heads, len(deps)),
        grid_spec=pltpu.PrefetchScalarGridSpec(
            num_scalar_prefetch=1,
            grid=(windows, tiles),
            in_specs=[
                row_spec,
                pl.BlockSpec((tq, width), lambda w, i, n: (block(w, i) + skip, 0)),
                row_spec,
                pl.BlockSpec((heads, tq), lambda w, i, n: (0, block(w, i))),
                key_spec,
                key_spec,
                pl.BlockSpec((8, tq), lambda w, i, n: (0, block(w, i))),
            ]
            + [pl.BlockSpec(memory_space=pl.ANY)] * len(deps),
            out_specs=[row_spec, key_spec, key_spec],
            scratch_shapes=[
                pltpu.VMEM((HD, heads * tq), F32),
                pltpu.VMEM((chips_z, chip_len, HD), F32),
                pltpu.VMEM((chips_z, chip_len, HD), F32),
                pltpu.VMEM((tk, tq), F32),
                pltpu.VMEM((heads, 8, tq), F32),
                pltpu.VMEM((tk, heads * tq), BF16),
                pltpu.VMEM((tk, heads * tq), BF16),
                pltpu.VMEM((heads * tq, HD), BF16),
                pltpu.VMEM((heads * tq, HD), BF16),
                pltpu.VMEM((chips_z, HD, chip_len), BF16),
            ],
        ),
        out_shape=[jax.ShapeDtypeStruct((rows, width), BF16), key_shape, key_shape],
        compiler_params=pltpu.CompilerParams(vmem_limit_bytes=40 * 2**20),
        cost_estimate=estimate(
            flops=4 * rows * width * chip_len * chips_z, bytes_accessed=8 * rows * width,
            transcendentals=rows * heads * chip_len * chips_z // 4,
        ),
        name="attention_backward",
    )(nums, queries, grad_attended, attended, lse, keys, values, spread, *deps)


def tile_numbers(starts, positions, z, tq, tk):
    windows, local = starts.shape
    tiled = starts.reshape(windows, local // tq, tq)
    t0 = jnp.broadcast_to(positions.reshape(local // tq, tq)[None, :, 0], (windows, local // tq))
    first, last = tiled[:, :, 0], tiled[:, :, -1]
    return jnp.stack(
        [t0, first // tk, (t0 + tq - 1) // tk + 1, (last + tk - 1) // tk, (t0 + 1) // tk, jnp.broadcast_to(z, t0.shape)],
        axis=2,
    ).astype(jnp.int32)


def store(part, total, extras, outs):
    outs[0][part, :] = total.astype(outs[0].dtype)


def sum_finish(part, total, extras, outs):
    total = total + extras[0][part, :] + extras[1][...] + extras[2][part, :].astype(F32) + extras[3][part, :]
    outs[0][part, :] = total.astype(BF16)


def add_finish(part, total, extras, outs):
    outs[0][part, :] = (total + extras[0][part, :]).astype(outs[0].dtype)


def slope_finish(part, total, extras, outs):
    grad = (total * extras[0][part, :].astype(F32)).astype(BF16)
    outs[0][part, :] = grad
    sums = jnp.sum(grad.astype(F32).reshape(-1, 8, grad.shape[1]), axis=0)
    if part.start == 0:
        outs[1][...] = sums
    else:
        outs[1][...] += sums


def gelu_finish(part, total, extras, outs):
    u = total + extras[0][...]
    square = u * u
    s = 0.5 * jnp.tanh(u * (0.7978845608028654 + (0.7978845608028654 * 0.044715) * square)) + 0.5
    value = u * s
    outs[0][part, :] = value.astype(BF16)
    rate = 2 * 0.7978845608028654 + (6 * 0.7978845608028654 * 0.044715) * square
    outs[1][part, :] = (s + value * (1.0 - s) * rate).astype(BF16)


def rows_kernel(kind, chunk, extra_count, dep_count, finish, a_ref, b_ref, *refs):
    extras, outs = refs[:extra_count], refs[extra_count + dep_count :]
    dot = contract_cols if kind == "nt" else plain_dot
    for r in range(0, a_ref.shape[0], chunk):
        part = pl.ds(r, chunk)
        finish(part, dot(a_ref[part, :], b_ref[...]), extras, outs)


def matmul(
    kind, a, b, outs, finish=store, extras=(), tn=512, chunk=256, deps=(), depth=None, a_part=0, b_part=0, extra_part=0, name="matmul"
):
    m, k = a.shape[0], depth or a.shape[1]
    n = b.shape[0] if kind == "nt" else b.shape[1]
    tn, chunk = min(tn, n), min(chunk, m)
    skip = extra_part * (n // tn)
    given = {"tile": pl.BlockSpec((m, tn), lambda j: (0, j + skip)), "row": pl.BlockSpec((1, tn), lambda j: (0, j + skip))}
    spec = {"tile": pl.BlockSpec((m, tn), lambda j: (0, j)), "sums": pl.BlockSpec((8, tn), lambda j: (0, j))}
    shape = {"tile": (m, n), "sums": (8, n)}
    res = pl.pallas_call(
        functools.partial(rows_kernel, kind, chunk, len(extras), len(deps), finish),
        grid=(n // tn,),
        in_specs=[
            pl.BlockSpec((m, k), lambda j: (0, a_part)),
            pl.BlockSpec((tn, k), lambda j: (j, b_part)) if kind == "nt" else pl.BlockSpec((k, tn), lambda j: (0, j)),
        ]
        + [given[kind_of] for _, kind_of in extras]
        + [pl.BlockSpec(memory_space=pl.ANY)] * len(deps),
        out_specs=[spec[w] for _, w in outs],
        out_shape=[jax.ShapeDtypeStruct(shape[w], d) for d, w in outs],
        compiler_params=pltpu.CompilerParams(vmem_limit_bytes=52 * 2**20),
        cost_estimate=estimate(flops=2 * m * n * k, bytes_accessed=2 * (m * k + n * k + m * n), transcendentals=0),
        name=name,
    )(a, b, *[array for array, _ in extras], *deps)
    return res[0] if len(outs) == 1 else res


def tokens_kernel(chunk, chips_z, dep_count, spot, a0_ref, a1_ref, b0_ref, b1_ref, *refs):
    out, first, second, left = refs[dep_count:]

    @pl.when(pl.program_id(0) == 0)
    def _():
        left[0] = jnp.transpose(a0_ref[...])
        left[1] = jnp.transpose(a1_ref[...])

    for r in range(0, left.shape[1], chunk):
        part = pl.ds(r, chunk)
        out[part, :] = (plain_dot(left[0, part, :], b0_ref[...]) + plain_dot(left[1, part, :], b1_ref[...])).astype(BF16)
    half = first.shape[2]
    y, x = spot[0], spot[1]
    for n in range(2):
        for z in range(chips_z):
            for sent, plane, part in ((first, (1 - y) * 2 + n, 0), (second, n * 2 + 1 - x, 1)):
                row = ((plane * chips_z + z) * 2 + part) * half
                sent[n, z] = out[pl.ds(pl.multiple_of(row, half), half), :]


def over_tokens(a, b, spot, chips_z, tn=512, chunk=256, deps=(), a_cols=None, name="weight_gradient"):
    k = a[0].shape[0]
    first, m = a_cols or (0, a[0].shape[1])
    n = b[0].shape[1]
    tn, chunk = min(tn, n), min(chunk, m)
    skip = first // m
    half = max(m // (8 * chips_z), 16)
    a_spec = pl.BlockSpec((k, m), lambda j, spot: (0, skip))
    b_spec = pl.BlockSpec((k, tn), lambda j, spot: (0, j))
    sent_spec = pl.BlockSpec((2, chips_z, half, tn), lambda j, spot: (0, 0, 0, j))
    sent_shape = jax.ShapeDtypeStruct((2, chips_z, half, n), BF16)
    total, *sent = pl.pallas_call(
        functools.partial(tokens_kernel, chunk, chips_z, len(deps)),
        grid_spec=pltpu.PrefetchScalarGridSpec(
            num_scalar_prefetch=1,
            grid=(n // tn,),
            in_specs=[a_spec, a_spec, b_spec, b_spec] + [pl.BlockSpec(memory_space=pl.ANY)] * len(deps),
            out_specs=[pl.BlockSpec((m, tn), lambda j, spot: (0, j)), sent_spec, sent_spec],
            scratch_shapes=[pltpu.VMEM((2, m, k), BF16)],
        ),
        out_shape=[jax.ShapeDtypeStruct((m, n), BF16), sent_shape, sent_shape],
        compiler_params=pltpu.CompilerParams(vmem_limit_bytes=56 * 2**20),
        cost_estimate=estimate(flops=4 * m * n * k, bytes_accessed=4 * (m * k + n * k + m * n), transcendentals=0),
        name=name,
    )(spot, *a, *b, *deps)
    return total, tuple(sent)


def contract_rows(left_op, right_op):
    return lax.dot_general(left_op, right_op, (((0,), (0,)), ((), ())), preferred_element_type=F32)


def contract_cols(left_op, right_op):
    return lax.dot_general(left_op, right_op, (((1,), (1,)), ((), ())), preferred_element_type=F32)


def plain_dot(left_op, right_op):
    return jnp.dot(left_op, right_op, preferred_element_type=F32)


def normalise(values):
    centred = values - jnp.mean(values, axis=-1, keepdims=True)
    spread = jnp.mean(centred * centred, axis=-1, keepdims=True)
    inverse = lax.rsqrt(spread + 1e-05)
    return centred * inverse, inverse


def norm_kernel(rounded, dep_count, own_ref, got_ref, unit_ref, inverse_ref, gain_ref, base_ref, *refs):
    outs = refs[dep_count:]
    grad = own_ref[...] + got_ref[...].astype(F32)
    unit = unit_ref[...]
    scaled = grad * gain_ref[...]
    inner = jnp.mean(scaled * unit, axis=-1, keepdims=True)
    level = jnp.mean(scaled, axis=-1, keepdims=True)
    result = base_ref[...].astype(F32) + (scaled - level - unit * inner) * inverse_ref[...][:, :1]
    outs[0][...] = result
    terms = [grad * unit, grad]
    if rounded:
        low = result.astype(BF16)
        outs[3][...] = low
        terms.append(low.astype(F32))
    first = pl.program_id(0) == 0
    for term, out in zip(terms, (outs[1], outs[2], outs[-1])):
        sums = jnp.sum(term.reshape(-1, 8, term.shape[1]), axis=0)

        @pl.when(first)
        def _(out=out, sums=sums):
            out[...] = sums

        @pl.when(jnp.logical_not(first))
        def _(out=out, sums=sums):
            out[...] += sums


def norm_backward(own, got, unit, inverse, gain, base, rounded, deps=()):
    rows, cols = own.shape
    tile = min(128, rows)
    block = pl.BlockSpec((tile, cols), lambda i: (i, 0))
    sums = pl.BlockSpec((8, cols), lambda i: (0, 0))
    sums_shape = jax.ShapeDtypeStruct((8, cols), F32)
    out_specs, out_shape = [block, sums, sums], [jax.ShapeDtypeStruct((rows, cols), F32), sums_shape, sums_shape]
    if rounded:
        out_specs += [block, sums]
        out_shape += [jax.ShapeDtypeStruct((rows, cols), BF16), sums_shape]
    return pl.pallas_call(
        functools.partial(norm_kernel, rounded, len(deps)),
        grid=(rows // tile,),
        in_specs=[
            block, block, block, pl.BlockSpec((tile, HD), lambda i: (i, 0)), pl.BlockSpec((1, cols), lambda i: (0, 0)), block,
        ]
        + [pl.BlockSpec(memory_space=pl.ANY)] * len(deps),
        out_specs=out_specs,
        out_shape=out_shape,
        compiler_params=pltpu.CompilerParams(vmem_limit_bytes=40 * 2**20),
        name="norm_backward",
    )(own, got, unit, jnp.broadcast_to(inverse, (rows, HD)), gain.reshape(1, cols), base, *deps)


def swap(values, axis):
    return lax.ppermute(values, axis, PAIR)


def in_order(index, own, other):
    return jnp.where(index == 0, jnp.stack([own, other]), jnp.stack([other, own]))


def pick(values, index, axis):
    return lax.dynamic_index_in_dim(values, index, axis, keepdims=False)


def exchange_add(values, index, axis_name, dim):
    arrived = swap(pick(values, 1 - index, dim), axis_name)
    return pick(values, index, dim).astype(F32) + arrived.astype(F32)


def core_rows(core, first, second):
    own = jnp.where(core == 0, first, second)
    other = swap(jnp.where(core == 0, second, first), "core")
    return in_order(core, own, other).reshape(2 * own.shape[0], own.shape[1])


def hold_kernel(dep_count, value_ref, *refs):
    refs[dep_count][...] = value_ref[...]


def hold(value, *deps):
    whole = pl.BlockSpec(value.shape, lambda: (0,) * value.ndim)
    return pl.pallas_call(
        functools.partial(hold_kernel, len(deps)),
        in_specs=[whole] + [pl.BlockSpec(memory_space=pl.ANY)] * len(deps),
        out_specs=whole,
        out_shape=jax.ShapeDtypeStruct(value.shape, value.dtype),
        name="hold",
    )(value, *deps)


def add_kernel(first, second, *refs):
    refs[-1][...] = (first[...].astype(F32) + second[...].astype(F32)).astype(BF16)


def add_after(first, second, *deps):
    whole = pl.BlockSpec(first.shape, lambda: (0,) * first.ndim)
    return pl.pallas_call(
        add_kernel,
        in_specs=[whole] * 2 + [pl.BlockSpec(memory_space=pl.ANY)] * len(deps),
        out_specs=whole,
        out_shape=jax.ShapeDtypeStruct(first.shape, BF16),
        name="add_after",
    )(first, second, *deps)


def place_kernel(moves_of, whole_count, half, dep_count, spot, *refs):
    count = len(moves_of)
    pieces = refs[:count]
    whole = refs[count : count + whole_count]
    out, held, arrive, leave = refs[count + whole_count + dep_count :]
    y, x, z = spot[0], spot[1], spot[2]
    steps = count // 4
    parts = 2 + whole_count * 2
    moves = []
    for n, move in enumerate(moves_of):
        s, k = move
        from_z = lax.rem(z - s + steps, steps)
        for i in range(2):
            to = ((i, x, 0), (i, 1 - x, 0), (y, i, 1), (1 - y, i, 1))[k]
            row = (((to[0] * 2 + to[1]) * steps + from_z) * parts + whole_count * 2 + to[2]) * half
            moves.append((pieces[n].at[i], pl.multiple_of(row, half), half))
    for array in whole:
        for chip in range(4 * steps):
            moves.append((array.at[pl.ds(chip * 2 * half, 2 * half), :], chip * parts * half, 2 * half))
    inward, outward, at = [], [], 0
    for n, (source, row, rows) in enumerate(moves):
        here = held.at[pl.ds(at, rows), :]
        inward.append(pltpu.make_async_copy(source, here, arrive.at[n]))
        outward.append(pltpu.make_async_copy(here, out.at[pl.ds(row, rows), :], leave.at[n]))
        at += rows
    for copy in inward:
        copy.start()
    for n, copy in enumerate(inward):
        copy.wait()
        outward[n].start()
    for copy in outward:
        copy.wait()


def place(pieces, spot, whole=(), deps=()):
    steps = len(pieces) // 4
    _, half, cols = pieces[0].shape
    count = 8 * steps + 4 * steps * len(whole)
    rows = 8 * steps * half * (1 + len(whole))
    moves_of = [(s, k) for s in range(steps) for k in range(4)]
    return pl.pallas_call(
        functools.partial(place_kernel, moves_of, len(whole), half, len(deps)),
        grid_spec=pltpu.PrefetchScalarGridSpec(
            num_scalar_prefetch=1,
            grid=(1,),
            in_specs=[pl.BlockSpec(memory_space=pl.ANY)] * (len(pieces) + len(whole) + len(deps)),
            out_specs=pl.BlockSpec(memory_space=pl.ANY),
            scratch_shapes=[
                pltpu.VMEM((rows, cols), BF16),
                pltpu.SemaphoreType.DMA((count,)),
                pltpu.SemaphoreType.DMA((count,)),
            ],
        ),
        out_shape=jax.ShapeDtypeStruct((rows, cols), BF16),
        compiler_params=pltpu.CompilerParams(vmem_limit_bytes=32 * 2**20),
        name="place_weight",
    )(spot, *pieces, *whole, *deps)


def gather_pieces(block, y, x, chips_z):
    half = block.shape[0] // 2
    ring = [(i, (i + 1) % chips_z) for i in range(chips_z)]
    one, two = block[:half], block[half:]
    got_one, got_two = swap(one, "y"), swap(two, "x")
    one, two = in_order(y, one, got_one), in_order(x, two, got_two)
    pieces, stages = [], []
    for s in range(chips_z):
        stages.append((one, two))
        pieces += [one, swap(one, "x"), two, swap(two, "y")]
        if s < chips_z - 1:
            one, two = lax.ppermute(one, "z", ring), lax.ppermute(two, "z", ring)
    return pieces, stages


def fold_kernel(spot, own_one, own_two, got_one, got_two, *refs):
    keep_one, send_one, keep_two, send_two = refs[-4:]
    y, x = spot[0], spot[1]
    for mine, own, got, keep, send in ((x, own_one, got_one, keep_one, send_one), (y, own_two, got_two, keep_two, send_two)):
        for index, out in ((mine, keep), (1 - mine, send)):
            total = own[own_at(own, index)].astype(F32) + got[index, 0].astype(F32)
            out[0] = total.astype(BF16)


def own_at(ref, index):
    return (index, 0, 0, 0) if ref.shape[0] == 2 else (0, index, 0, 0)


def fold_again_kernel(count, *refs):
    out = refs[-1]
    cols = out.shape[-1] // count
    for n in range(count):
        keep_one, keep_two, got_one, got_two = refs[4 * n : 4 * n + 4]
        here = pl.ds(n * cols, cols)
        out[0, 0, :, here] = (keep_one[0].astype(F32) + got_one[0].astype(F32)).astype(BF16)
        out[0, 1, :, here] = (keep_two[0].astype(F32) + got_two[0].astype(F32)).astype(BF16)


class Sum:
    def __init__(self, total, sent, spot, chips_z):
        self.cols = total.shape[1]
        self.half = total.shape[0] // (8 * chips_z)
        self.total, self.spot, self.chips_z = total.reshape(2, 2, chips_z, 2, self.half, self.cols), spot, chips_z
        self.sent = sent

    def first(self, *deps):
        got = (swap(self.sent[0], "y"), swap(self.sent[1], "x"))
        block = (self.half, self.cols)
        got_spec = pl.BlockSpec((2, 1, *block), lambda z, spot: (0, z, 0, 0))
        out_spec = pl.BlockSpec((1, *block), lambda z, spot: (z, 0, 0))
        keep_one, send_one, keep_two, send_two = pl.pallas_call(
            fold_kernel,
            grid_spec=pltpu.PrefetchScalarGridSpec(
                num_scalar_prefetch=1,
                grid=(self.chips_z,),
                in_specs=[
                    pl.BlockSpec((1, 2, 1, 1, *block), lambda z, spot: (spot[0], 0, z, 0, 0, 0)),
                    pl.BlockSpec((2, 1, 1, 1, *block), lambda z, spot: (0, spot[1], z, 1, 0, 0)),
                    got_spec,
                    got_spec,
                ]
                + [pl.BlockSpec(memory_space=pl.ANY)] * len(deps),
                out_specs=[out_spec] * 4,
            ),
            out_shape=[jax.ShapeDtypeStruct((self.chips_z, *block), BF16)] * 4,
            compiler_params=pltpu.CompilerParams(vmem_limit_bytes=32 * 2**20),
            name="fold",
        )(self.spot, self.total, self.total, *got, *deps)
        self.keep, self.sent = (keep_one, keep_two), (send_one, send_two)

    def second(self, *deps, beside=()):
        sums = (self, *beside)
        arrays = []
        for one in sums:
            arrays += [*one.keep, swap(one.sent[0], "x"), swap(one.sent[1], "y")]
        self.cols *= len(sums)
        self.both = pl.pallas_call(
            functools.partial(fold_again_kernel, len(sums)),
            grid=(self.chips_z,),
            in_specs=[pl.BlockSpec((1, *array.shape[1:]), lambda z: (z, 0, 0)) for array in arrays]
            + [pl.BlockSpec(memory_space=pl.ANY)] * len(deps),
            out_specs=pl.BlockSpec((1, 2, self.half, self.cols), lambda z: (z, 0, 0, 0)),
            out_shape=jax.ShapeDtypeStruct((self.chips_z, 2, self.half, self.cols), BF16),
            compiler_params=pltpu.CompilerParams(vmem_limit_bytes=32 * 2**20),
            name="fold_again",
        )(*arrays, *deps).reshape(-1, self.cols)

    def round_z(self, ring):
        z = self.spot[2]
        both = self.both.reshape(self.chips_z, -1, self.cols)
        running = pick(both, (z + self.chips_z - 1) % self.chips_z, 0)
        for s in range(2, self.chips_z + 1):
            mine = pick(both, (z + self.chips_z - s) % self.chips_z, 0)
            total = mine.astype(F32) + lax.ppermute(running, "z", ring).astype(F32)
            running = total.astype(BF16)
        return total

    def over_z(self):
        self.result = lax.psum_scatter(self.both, "z", scatter_dimension=0, tiled=True)
        return self.result.astype(F32)


def pack_kernel(spot, gain1, bias1, query0, query1, out_bias, gain2, bias2, down_bias, *refs):
    *units, packed = refs
    width = packed.shape[1]
    core = spot[0]
    packed[...] = jnp.zeros_like(packed)
    for n, ref in enumerate((gain1, bias1, out_bias, gain2, bias2, down_bias)):
        packed[n : n + 1, :] = jnp.sum(ref[...], axis=0, keepdims=True)
    count = len(units) // 2
    for n in range(count):
        total = units[2 * n][...] + units[2 * n + 1][...]
        packed[pl.ds(8 + core * count + n, 1), : total.shape[1]] = jnp.sum(total, axis=0, keepdims=True)
    columns = jnp.sum(query0[...], axis=0, keepdims=True) + jnp.sum(query1[...], axis=0, keepdims=True)
    half = width // 2
    for n in range(2):
        packed[6:7, n * half : (n + 1) * half] = jnp.where(core == n, columns[:, :half], 0.0)
    packed[7:8, :HD] = jnp.where(core == 0, 0.0, columns[:, half:])


def pack(core, *arrays):
    width = arrays[0].shape[1]
    units = (len(arrays) - 8) // 2
    return pl.pallas_call(
        pack_kernel,
        grid_spec=pltpu.PrefetchScalarGridSpec(
            num_scalar_prefetch=1,
            grid=(1,),
            in_specs=[pl.BlockSpec(a.shape, lambda i, spot: (0, 0)) for a in arrays],
            out_specs=pl.BlockSpec((8 + 2 * units, width), lambda i, spot: (0, 0)),
        ),
        out_shape=jax.ShapeDtypeStruct((8 + 2 * units, width), F32),
        compiler_params=pltpu.CompilerParams(vmem_limit_bytes=32 * 2**20),
        name="pack_small",
    )(core.reshape(1).astype(jnp.int32), *arrays)


def doubling(axis):
    size = lax.axis_size(axis)
    step = 1
    while step < size:
        yield step, [(i, i ^ step) for i in range(size)]
        step *= 2


def gather_small(vector):
    for axis in reversed(EVERY):
        index = lax.axis_index(axis)
        for step, pairs in doubling(axis):
            vector = in_order((index // step) % 2, vector, lax.ppermute(vector, axis, pairs))
    return vector.reshape(-1, vector.shape[-1])


def gather_rows(block):
    rows = block[None]
    for axis in reversed(CHIPS):
        index = lax.axis_index(axis)
        for step, pairs in doubling(axis):
            rows = in_order((index // step) % 2, rows, lax.ppermute(rows, axis, pairs))
            rows = rows.reshape(-1, *block.shape)
    return rows.reshape(-1, block.shape[1])


def sum_small(vector):
    for axis in reversed(EVERY):
        for _, pairs in doubling(axis):
            vector = vector + lax.ppermute(vector, axis, pairs)
    return vector


def join_kernel(cut, core, own, other, out):
    cols = own.shape[1]
    rest = cols - cut
    for n in range(2):
        for index, ref in ((n, own), (1 - n, other)):

            @pl.when(core[0] == n)
            def _(index=index, ref=ref):
                out[:, index * cut : (index + 1) * cut] = ref[:, :cut]
                out[:, 2 * cut + index * rest : 2 * cut + (index + 1) * rest] = ref[:, cut:]


def join_columns(core, own, other, cut):
    rows, cols = own.shape
    whole = pl.BlockSpec((rows, cols), lambda i, spot: (0, 0))
    return pl.pallas_call(
        functools.partial(join_kernel, cut),
        grid_spec=pltpu.PrefetchScalarGridSpec(
            num_scalar_prefetch=1,
            grid=(1,),
            in_specs=[whole, whole],
            out_specs=pl.BlockSpec((rows, 2 * cols), lambda i, spot: (0, 0)),
        ),
        out_shape=jax.ShapeDtypeStruct((rows, 2 * cols), F32),
        name="join_columns",
    )(core.reshape(1).astype(jnp.int32), own, other)


def own_rows(core, rows):
    pair = rows.reshape(2, rows.shape[0] // 2, rows.shape[1])
    own = pick(pair, core, 0)
    other = swap(pick(pair, 1 - core, 0), "core")
    return in_order(core, own, other)


def body(
    hidden_in, doc_lengths, cotangent, ln1_gain, ln1_bias, w_qkv, b_qv, w_out, b_out,
    ln2_gain, ln2_bias, w_up, b_up, w_down, b_down,
):
    windows, local_len, width = hidden_in.shape
    own_count = windows * local_len
    count = 2 * own_count
    chips_z = lax.axis_size("z")
    chips = 2 * lax.axis_size("y") * chips_z
    y, x, z, core = (lax.axis_index(name) for name in EVERY)
    width_q = HEADS * HD
    half_q = width_q // 2
    chip_len = 2 * local_len
    length = chip_len * chips_z
    hidden_units = w_up.shape[1]
    unit_block = hidden_units // (2 * chips)

    doc_ends = jnp.cumsum(doc_lengths, axis=1)
    cores = jnp.stack([core, 1 - core])
    positions = (z * chip_len + cores[:, None] * local_len + jnp.arange(local_len, dtype=jnp.int32)[None, :]).astype(jnp.int32)
    ended = positions[:, None, :, None] >= doc_ends[None, :, None, :]
    starts = jnp.max(jnp.where(ended, doc_ends[None, :, None, :], 0), axis=3)
    valid = (jnp.sum(ended[0].astype(jnp.int32), axis=2) < DOCS).reshape(own_count, 1)

    vectors = (ln1_gain, ln1_bias, b_qv, b_out, ln2_gain, ln2_bias, b_up, b_down)
    sizes = [v.shape[0] for v in vectors]
    packed = gather_small(jnp.concatenate(vectors)).astype(F32)
    full = []
    at = 0
    for size in sizes:
        full.append(packed[:, at : at + size].reshape(-1))
        at += size
    gain1, bias1, bias_qv, bias_out, gain2, bias2, bias_up, bias_down = full
    bias_up = jnp.swapaxes(pick(bias_up.reshape(chips, 2, 2, unit_block // 2), core, 1), 0, 1).reshape(-1)
    bias_qkv = jnp.where(
        core == 0,
        jnp.concatenate([bias_qv[:half_q], jnp.zeros((HD,), F32)]),
        jnp.concatenate([bias_qv[half_q:width_q], bias_qv[width_q:]]),
    )
    w_out_t = w_out.T
    near_block = core_rows(
        core,
        jnp.concatenate([w_qkv[:, :half_q], w_qkv[:, width_q : width_q + HD], w_out_t[:, :half_q]], axis=1),
        jnp.concatenate([w_qkv[:, half_q:width_q], w_qkv[:, width_q + HD :], w_out_t[:, half_q:]], axis=1),
    )
    up_parts = jnp.moveaxis(w_up.reshape(w_up.shape[0], chips, 2, 2, unit_block // 2), 3, 1)
    up_block = core_rows(
        core,
        up_parts[:, :, :, 0].reshape(w_up.shape[0], -1),
        up_parts[:, :, :, 1].reshape(w_up.shape[0], -1),
    )
    spot = jnp.stack([y, x, z]).astype(jnp.int32)
    by_hand = lax.axis_size("y") == 2
    ring = [(i, (i + 1) % chips_z) for i in range(chips_z)]

    def gather(block):
        return lax.all_gather(block, CHIPS, axis=0, tiled=True)

    def both_cores(own):
        return (own, swap(own, "core"))

    near_all, w_up_all = gather(near_block), gather(up_block)
    w_out_all = near_all[:, half_q + HD :]

    tokens = hidden_in.reshape(own_count, width).astype(F32)
    unit1, inverse1 = normalise(tokens)
    normed1 = both_cores((unit1 * gain1 + bias1).astype(BF16))
    w_query, w_kv = near_all[:, :half_q], gather_rows(near_block[:, half_q : half_q + HD])
    own_kv = [(plain_dot(rows, w_kv) + bias_qkv[half_q:]).astype(BF16) for rows in normed1]
    own_kv = [rows.reshape(windows, local_len, HD) for rows in own_kv]
    own_kv = jnp.swapaxes(in_order(core, *own_kv), 0, 1).reshape(windows, chip_len, HD)
    keys, values = [], []
    for s in range(chips_z):
        other_kv = swap(own_kv, "core")
        keys.append(jnp.where(core == 0, own_kv, other_kv))
        values.append(jnp.where(core == 0, other_kv, own_kv))
        if s < chips_z - 1:
            own_kv = lax.ppermute(own_kv, "z", ring)
    down_rows = w_down.shape[0] // 2
    w_down_parts = [gather(w_down[:down_rows]), gather(w_down[down_rows:])]
    keys, values = jnp.stack(keys), jnp.stack(values)
    queries = [(plain_dot(rows, w_query) + bias_qkv[:half_q]).astype(BF16) for rows in normed1]
    tq_forward, tk_forward = min(512, local_len), min(512, chip_len)
    tq, tk = min(256, local_len), min(256, chip_len)
    attended, lse = [None, None], [None, None]
    for n in (1, 0):
        attended[n], lse[n] = attend_forward(
            queries[n], keys, values, starts[n],
            tile_numbers(starts[n], positions[n], z, tq_forward, tk_forward), tq_forward, tk_forward,
            () if n == 1 else (attended[1],),
        )
        if n == 1:
            out_other = swap(matmul("nt", attended[1], w_out_all, [(BF16, "tile")], name="attention_out"), "core")
    residual = tokens + bias_out + contract_cols(attended[0], w_out_all) + out_other.astype(F32)

    unit2, inverse2 = normalise(residual)
    normed2 = both_cores((unit2 * gain2 + bias2).astype(BF16))
    active, slope = [None, None], [None, None]
    for n in (0, 1):
        active[n], slope[n] = matmul(
            "nn", normed2[n], w_up_all, [(BF16, "tile"), (BF16, "tile")], gelu_finish, [(bias_up.reshape(1, -1), "row")],
            name="upward",
        )
    upstream = jnp.where(valid, cotangent.reshape(own_count, width), 0)
    grad_down = both_cores(upstream)
    units = active[0].shape[1] // 2
    down_totals = [
        over_tokens(active, grad_down, spot, chips_z, a_cols=(n * units, units), name="grad_w_down") for n in (0, 1)
    ]
    down_sums = [Sum(*total, spot, chips_z) for total in down_totals] if by_hand else ()
    down_totals = [total for total, _ in down_totals]

    grad_up, unit_sums, up_totals, up_sums = [None, None], [], [], []
    grad_normed, down_out = [None, None], [None, None]
    deps = tuple(array for one in down_sums for array in one.sent)
    for part in (0, 1):
        for n in (0, 1):
            grad_up[n], sums = matmul(
                "nt", grad_down[n], w_down_parts[part], [(BF16, "tile"), (F32, "sums")], slope_finish, [(slope[n], "tile")],
                extra_part=part, deps=deps, name="grad_up",
            )
            unit_sums.append(sums)
        total, sent = over_tokens(normed2, grad_up, spot, chips_z, name="grad_w_up")
        up_totals.append(total)
        deps = (up_totals[-1],)
        if by_hand:
            up_sums.append(Sum(total, sent, spot, chips_z))
            deps += up_sums[-1].sent
            if part == 1:
                down_sums[0].second(up_totals[1], beside=down_sums[1:])
                grad_w_down = down_sums[0].over_z()
                deps += (down_sums[0].both,)
        for n in (1, 0):
            grad_normed[n] = matmul(
                "nt", grad_up[n], w_up_all, [(F32 if n == 0 or part == 0 else BF16, "tile")],
                add_finish if part else store, [(grad_normed[n], "tile")] if part else (), depth=units, b_part=part,
                deps=deps, name="grad_normed2",
            )
            deps = (grad_normed[n],)
        for n in (1, 0)[: 2 - part]:
            down_out[n] = matmul(
                "nn", active[n], w_down_parts[part], [(BF16 if part else F32, "tile")], add_finish if part else store,
                [(down_out[n], "tile")] if part else (), depth=units, a_part=part, deps=deps, name="mixed_out",
            )
            deps = (down_out[n],)
        if by_hand and part == 0:
            for one in down_sums:
                one.first(down_out[0])
            deps += tuple(array for one in down_sums for array in one.sent)
    mixed_other, mixed_own = grad_normed[1], grad_normed[0]
    down_other = down_out[1]
    grad_residual, gain2_sums, bias2_sums, branch_own, out_sums = norm_backward(
        mixed_own, swap(mixed_other, "core"), unit2, inverse2, gain2, upstream, True, deps
    )
    branch = both_cores(branch_own)

    grad_attended, deps = [], ()
    for n in (0, 1):
        grad_attended.append(matmul("nn", branch[n], w_out_all, [(BF16, "tile")], deps=deps, name="grad_attended"))
        if by_hand and n == 0:
            for one in up_sums:
                one.first(grad_attended[0])
                deps += one.sent
    grad_query, grad_keys, grad_values = [None, None], [None, None], [None, None]
    for n in (0, 1):
        deps = ()
        if by_hand:
            if n == 1:
                up_sums[0].second(grad_keys[0], beside=up_sums[1:])
                grad_w_up = up_sums[0].over_z()
                deps = (up_sums[0].both, down_sums[0].result)
        grad_query[n], grad_keys[n], grad_values[n] = attend_backward(
            queries[n], grad_attended[n], 0, attended[n], lse[n], keys, values, starts[n],
            tile_numbers(starts[n], positions[n], z, tq, tk), tq, tk, deps,
        )
    grad_keys = grad_keys[0].astype(F32) + grad_keys[1].astype(F32)
    grad_values = grad_values[0].astype(F32) + grad_values[1].astype(F32)
    kv_sent = jnp.where(core == 0, grad_values, grad_keys).astype(BF16)
    query_total, query_sent = over_tokens(normed1, grad_query, spot, chips_z, deps=(kv_sent,), name="grad_w_query")
    grad_kv = (jnp.where(core == 0, grad_keys, grad_values) + swap(kv_sent, "core").astype(F32)).astype(BF16)
    running = hold(grad_kv[1 % chips_z], query_total, *((up_sums[0].result,) if by_hand else ()))
    out_total, sent = over_tokens(branch, attended, spot, chips_z, deps=(running,), name="grad_w_out")
    if by_hand:
        out_sum = Sum(out_total, sent, spot, chips_z)
    deps = (out_total,)
    for s in range(2, chips_z + 1):
        running = add_after(grad_kv[s % chips_z], lax.ppermute(running, "z", ring), *deps)
        if s == 2:
            mixed_out = matmul(
                "nn", active[0], w_down_parts[1], [(BF16, "tile")], sum_finish,
                [(residual, "tile"), (bias_down.reshape(1, -1), "row"), (swap(down_other, "core"), "tile"), (down_out[0], "tile")],
                depth=units, a_part=1, deps=(running, *sent), name="mixed_out",
            )
            deps = (mixed_out,)
    grad_kv = jnp.swapaxes(running.reshape(windows, 2, local_len, HD), 0, 1)
    grad_kv = in_order(core, grad_kv[0], grad_kv[1]).reshape(2, own_count, HD)
    kv_total = (contract_rows(normed1[0], grad_kv[0]) + contract_rows(normed1[1], grad_kv[1])).astype(BF16)
    qkv_total = jnp.concatenate([query_total, kv_total], axis=1)
    grad_qkv = [jnp.concatenate([grad_query[n], grad_kv[n]], axis=1) for n in (0, 1)]
    deps = (mixed_out,)
    if by_hand:
        parts = kv_total.reshape(2, 2, chips_z, 2, -1, HD)
        kv_parts = (pick(parts[:, :, :, 0], 1 - y, 0), pick(parts[:, :, :, 1], 1 - x, 1))
        sent = tuple(jnp.concatenate(pair, axis=3) for pair in zip(query_sent, kv_parts))
        qkv_sum = Sum(qkv_total, sent, spot, chips_z)
        deps += qkv_sum.sent
    first_other = matmul("nt", grad_qkv[1], near_all, [(BF16, "tile")], deps=deps, name="grad_normed1")
    first_own = matmul("nt", grad_qkv[0], near_all, [(F32, "tile")], deps=(first_other,), name="grad_normed1")
    grad_hidden, gain1_sums, bias1_sums = norm_backward(
        first_own, swap(first_other, "core"), unit1, inverse1, gain1, grad_residual, False
    )
    if by_hand:
        qkv_sum.first(gain1_sums)
        out_sum.first(gain1_sums)
        qkv_sum.second(out_sum.sent[0])
        out_sum.second(qkv_sum.both)
        grad_w_out = out_sum.over_z()
        grad_w_qkv = qkv_sum.round_z(ring)
    qkv_sums = [jnp.sum(rows.astype(F32).reshape(-1, 8, rows.shape[1]), axis=0) for rows in grad_qkv]
    upstream_sums = jnp.sum(upstream.astype(F32).reshape(-1, 8, width), axis=0)

    if not by_hand:
        grad_w_down, grad_w_up, grad_w_out, grad_w_qkv = (
            lax.psum_scatter(total, CHIPS, scatter_dimension=0, tiled=True).astype(F32)
            for total in (jnp.concatenate(down_totals, axis=1), jnp.concatenate(up_totals, axis=1), out_total, qkv_total)
        )
    device = ((y * 2 + x) * chips_z + z) * 2 + core
    share = width // (2 * chips)
    sums = sum_small(
        pack(
            core, gain1_sums, bias1_sums, *qkv_sums, out_sums, gain2_sums, bias2_sums, upstream_sums, *unit_sums,
        )
    )
    vectors = lax.dynamic_slice(sums, (0, device * share), (7, share))
    value_bias = lax.dynamic_slice(sums, (7, device * (HD // (2 * chips))), (1, HD // (2 * chips)))[0]
    half_block = unit_block // 2
    unit_bias = lax.dynamic_slice(
        sums, (8 + 2 * core, ((y * 2 + x) * chips_z + z) * half_block), (2, half_block)
    ).reshape(-1)
    grad_w_down = jnp.concatenate([grad_w_down[:, :width], grad_w_down[:, width:]], axis=0)
    pair = grad_w_qkv.reshape(2, -1, half_q + HD)
    own_qkv = join_columns(core, pick(pair, core, 0), swap(pick(pair, 1 - core, 0), "core"), half_q)
    own_out = own_rows(core, grad_w_out)
    own_out = jnp.concatenate([own_out[0], own_out[1]], axis=1).T
    own_up = own_rows(core, grad_w_up)
    own_up = own_up.reshape(2, own_up.shape[1], 2, chips, half_block)
    own_up = jnp.transpose(own_up, (1, 3, 0, 2, 4)).reshape(own_up.shape[1], -1)
    return (
        mixed_out.reshape(windows, local_len, width),
        grad_hidden.reshape(windows, local_len, width),
        vectors[0], vectors[1], own_qkv, vectors[6], value_bias, own_out, vectors[2], vectors[3], vectors[4],
        own_up, unit_bias, grad_w_down, vectors[5],
    )


def solution(mesh):
    split = Mesh(mesh.devices.reshape(mesh.shape["dp"] // 2, 2, mesh.shape["seq"] // 2, 2), EVERY)
    rows = ("y", "x")
    cols = ("z", "core")
    vector, matrix = P(EVERY), P(EVERY, None)
    tokens = P(rows, cols, None)
    return jax.shard_map(
        body,
        mesh=split,
        in_specs=(
            tokens, P(rows, None), tokens, vector, vector, matrix, vector, P(None, EVERY), vector,
            vector, vector, matrix, vector, matrix, vector,
        ),
        out_specs=(
            tokens, tokens, vector, vector, matrix, vector, vector, P(None, EVERY), vector, vector, vector,
            matrix, vector, matrix, vector,
        ),
        check_vma=False,
    )
```
